32 devices in a mesh: seq: 8 (over y, x, core), tp: 4 (over z).
Axes of the slice: x: 2, y: 2, z: 4, core: 2. Of those that a mesh axis runs over, the one named last changes fastest.
Arguments:
- tokens: bfloat16 [12288, 1536], P(('seq', 'tp')), may hold values from -6 to 6
- cond_embed: bfloat16 [24, 1024], P('seq'), may hold values from -6 to 6
- caption: bfloat16 [6144, 4096], P(('seq', 'tp')), may hold values from -6 to 6
- clip_len: int32 [8, 3], P('seq'), may hold values from 1 to 1024, 1536 in all within a row
- rope_off: int32 [8, 3], P('seq'), may hold values from 0 to 2047
- text_len: int32 [8, 3], P('seq'), may hold values from 32 to 256
- query_proj: bfloat16 [1536, 1536], P(None, 'tp'), may hold values from -0.15625 to 0.15625
- key_proj: bfloat16 [1536, 1536], P(None, 'tp'), may hold values from -0.15625 to 0.15625
- value_proj: bfloat16 [1536, 1536], P(None, 'tp'), may hold values from -0.15625 to 0.15625
- out_proj: bfloat16 [1536, 1536], P('tp'), may hold values from -1.5 to 1.5
- gate_proj: bfloat16 [1536, 4096], P(None, 'tp'), may hold values from -0.15625 to 0.15625
- up_proj: bfloat16 [1536, 4096], P(None, 'tp'), may hold values from -0.15625 to 0.15625
- down_proj: bfloat16 [4096, 1536], P('tp'), may hold values from -0.09375 to 0.09375
- key_text: bfloat16 [4096, 1536], P(None, 'tp'), may hold values from -0.09375 to 0.09375
- value_text: bfloat16 [4096, 1536], P(None, 'tp'), may hold values from -0.09375 to 0.09375
- ada_weight: bfloat16 [1024, 6, 1536], P(None, None, 'tp'), may hold values from -0.1875 to 0.1875
- ada_bias: bfloat16 [6, 1536], P(None, 'tp'), may hold values from -1.5 to 1.5
- query_gain: bfloat16 [24, 64], P('tp'), may hold values from 0.25 to 1.75
- key_gain: bfloat16 [24, 64], P('tp'), may hold values from 0.25 to 1.75
- text_gain: bfloat16 [24, 64], P('tp'), may hold values from 0.25 to 1.75
- text_gate: bfloat16 [24], P('tp'), may hold values from 0.29882812 to 1.1953125
- cotangent: bfloat16 [12288, 1536], P(('seq', 'tp')), may hold values from -6 to 6
Outputs:
- output: bfloat16 [12288, 1536], P(('seq', 'tp'))
- grad_tokens: bfloat16 [12288, 1536], P(('seq', 'tp'))
- grad_query_proj: float32 [1536, 1536], P('seq', 'tp')
- grad_key_proj: float32 [1536, 1536], P('seq', 'tp')
- grad_value_proj: float32 [1536, 1536], P('seq', 'tp')
- grad_out_proj: float32 [1536, 1536], P('tp', 'seq')
- grad_gate_proj: float32 [1536, 4096], P('seq', 'tp')
- grad_up_proj: float32 [1536, 4096], P('seq', 'tp')
- grad_down_proj: float32 [4096, 1536], P('tp', 'seq')
- grad_key_text: float32 [4096, 1536], P('seq', 'tp')
- grad_value_text: float32 [4096, 1536], P('seq', 'tp')
- grad_ada_weight: float32 [1024, 6, 1536], P('seq', None, 'tp')
- grad_ada_bias: float32 [6, 1536], P(None, 'tp')
- grad_query_gain: float32 [24, 64], P('tp')
- grad_key_gain: float32 [24, 64], P('tp')
- grad_text_gain: float32 [24, 64], P('tp')
- grad_text_gate: float32 [24], P('tp')
The draws below stay inside these ranges and needn't reach their ends.
All inputs are finite; a program needn't handle non-finite values.
Results may differ from the reference program's by a relative error of at most 0.014.
Values may be sent and summed in bfloat16 or wider, within the bound.
A program may use at most 256 MiB of HBM per device.

```python
import math
import jax
import jax.numpy as jnp
import numpy as np
from jax import lax

D = 1536
HEADS = 24
HEAD = 64
FF = 4096
TXT_D = 4096
COND = 1024
TXT = 256
CLIPS = 3
GROUP = 1536
TOKENS = 12288
LONGEST = 1024
N_SEQ = 8


def touch_ends(drawn, own_key, smallest, largest):
    index_at = [jax.random.randint(jax.random.fold_in(own_key, axis), (), 0, length) for axis, length in enumerate(drawn.shape)]
    longest = drawn.shape.index(max(drawn.shape))
    neighbour = index_at[:longest] + [(index_at[longest] + 1) % drawn.shape[longest]] + index_at[longest + 1:]
    return drawn.at[tuple(index_at)].set(smallest).at[tuple(neighbour)].set(largest)


def level_of(key, extent, split, smallest, largest):
    factor_of = 1.0
    for axis_at, shards_of in split:
        draws = jax.random.uniform(jax.random.fold_in(jax.random.fold_in(key, 6), axis_at), (shards_of,), jnp.float32, smallest / len(split), largest / len(split))
        factor_of = factor_of * jnp.repeat(jnp.exp(draws), extent[axis_at] // shards_of).reshape((-1,) + (1,) * (len(extent) - 1 - axis_at))
    return factor_of


def profile(count, total, reach, skew):
    weights = [(1 << 20) // math.isqrt(standing ** skew) + 1 for standing in range(2, count + 1)]
    rest, holding = total - reach - (count - 1), [1] * (count - 1)
    while rest > 0:
        candidates = [i for i in range(count - 1) if holding[i] < reach]
        whole, remaining = sum([weights[i] for i in candidates]), rest
        for i in candidates:
            extra = min(reach - holding[i], max(1, remaining * weights[i] // whole), rest)
            holding[i] = holding[i] + extra
            rest = rest - extra
    return np.array([reach] + holding)


def ragged(key, count, total, most, slope):
    if count == 2:
        one = jax.random.randint(key, (), max(1, total - most), min(most, total - 1) + 1)
        return jnp.stack([one, total - one])
    sizes = jnp.asarray(profile(count, total, most, slope), jnp.int32)
    pairs = (count - 1) // 2
    donor, receiver = sizes[1:1 + 2 * pairs:2], sizes[2:2 + 2 * pairs:2]
    slack = jnp.minimum(donor - 1, most - receiver)
    passed = jax.random.randint(jax.random.fold_in(key, 1), (pairs,), 0, 1 << 20) % (slack + 1)
    sizes = sizes.at[1:1 + 2 * pairs:2].set(donor - passed).at[2:2 + 2 * pairs:2].set(receiver + passed)
    return sizes[jax.random.permutation(jax.random.fold_in(key, 2), count)]


def bell_draw(own_key, shape, width, most, cuts=(), kind=jnp.bfloat16):
    level = level_of(own_key, shape, cuts, -0.22, 0.18) if cuts else 1.0
    values = jax.random.normal(own_key, shape, jnp.float32) * width * level
    return jnp.minimum(jnp.maximum(values, -most), most).astype(kind)


def setup_inputs(seed: int = 0) -> dict:
    streams_of = jax.random.split(jax.random.key(seed), 23)
    return {
        "tokens": bell_draw(streams_of[0], (TOKENS, D), 1.0, 6.0, ((0, 32),)),
        "cond_embed": bell_draw(streams_of[1], (N_SEQ * CLIPS, COND), 1.0, 6.0, ((0, 8),)),
        "caption": bell_draw(streams_of[2], (N_SEQ * CLIPS * TXT, TXT_D), 1.0, 6.0, ((0, 32),)),
        "clip_len": jax.vmap(lambda own: ragged(own, CLIPS, GROUP, LONGEST, 2))(jax.random.split(streams_of[3], N_SEQ)).reshape((N_SEQ, CLIPS)).astype(jnp.int32),
        "rope_off": touch_ends(jax.random.randint(streams_of[4], (N_SEQ, CLIPS), 0, 2048), jax.random.fold_in(streams_of[4], 1), 0, 2047).astype(jnp.int32),
        "text_len": touch_ends(jax.random.randint(streams_of[5], (N_SEQ, CLIPS), TXT // 8, TXT + 1), jax.random.fold_in(streams_of[5], 1), TXT // 8, TXT).astype(jnp.int32),
        "query_proj": bell_draw(streams_of[6], (D, D), D ** -0.5, 0.15625, ((1, 4),)),
        "key_proj": bell_draw(streams_of[7], (D, D), D ** -0.5, 0.15625, ((1, 4),)),
        "value_proj": bell_draw(streams_of[8], (D, D), D ** -0.5, 0.15625, ((1, 4),)),
        "out_proj": bell_draw(streams_of[9], (D, D), (max(1, D // 96)) ** -0.5, 1.5, ((0, 4),)),
        "gate_proj": bell_draw(streams_of[10], (D, FF), D ** -0.5, 0.15625, ((1, 4),)),
        "up_proj": bell_draw(streams_of[11], (D, FF), D ** -0.5, 0.15625, ((1, 4),)),
        "down_proj": bell_draw(streams_of[12], (FF, D), FF ** -0.5, 0.09375, ((0, 4),)),
        "key_text": bell_draw(streams_of[13], (TXT_D, D), TXT_D ** -0.5, 0.09375, ((1, 4),)),
        "value_text": bell_draw(streams_of[14], (TXT_D, D), TXT_D ** -0.5, 0.09375, ((1, 4),)),
        "ada_weight": bell_draw(streams_of[15], (COND, 6, D), COND ** -0.5, 0.1875, ((2, 4),)),
        "ada_bias": bell_draw(streams_of[16], (6, D), 0.3, 1.5, ((1, 4),)),
        "query_gain": jnp.clip(1.0 + 0.15 * jax.random.normal(streams_of[17], (HEADS, HEAD), jnp.float32), 0.25, 1.75).astype(jnp.bfloat16),
        "key_gain": jnp.clip(1.0 + 0.15 * jax.random.normal(streams_of[18], (HEADS, HEAD), jnp.float32), 0.25, 1.75).astype(jnp.bfloat16),
        "text_gain": jnp.clip(1.0 + 0.15 * jax.random.normal(streams_of[19], (HEADS, HEAD), jnp.float32), 0.25, 1.75).astype(jnp.bfloat16),
        "text_gate": jnp.clip(0.29882812 + 0.8964844 * jax.random.uniform(streams_of[20], (HEADS,), jnp.float32) ** level_of(streams_of[20], (HEADS,), ((0, 4),), -0.2, 0.2), 0.29882812, 1.1953125).astype(jnp.bfloat16),
        "cotangent": bell_draw(streams_of[21], (TOKENS, D), 1.0, 6.0, ((0, 32),)),
    }


epsilon = 1e-06
highest = lax.Precision.HIGHEST

@jax.custom_vjp
def low(v):
    return lax.optimization_barrier(v.astype(jnp.bfloat16)).astype(jnp.float32)

@jax.custom_vjp
def low_back(v):
    return v

def low_keep(v):
    return (low(v), None)

def low_pass(kept, grad):
    return (grad,)

def back_keep(v):
    return (v, None)

def back_low(kept, grad):
    return (low(grad),)
low.defvjp(low_keep, low_pass)
low_back.defvjp(back_keep, back_low)

def rms(values):
    return values * lax.rsqrt(lax.optimization_barrier(jnp.mean(values * values, axis=-1, keepdims=True)) + epsilon)

def rotate(values, cosine, sine):
    half = values.shape[-1] // 2
    first = values[..., :half]
    second = values[..., half:]
    return jnp.concatenate([first * cosine - second * sine, first * sine + second * cosine], axis=-1)

def attend(queries, keys, values, allowed, scale):
    scores = low_back(scale * jnp.einsum('sqd,skd->sqk', queries, keys, precision=highest))
    scores = jnp.where(allowed, scores, -1e+30)
    top = lax.optimization_barrier(jnp.max(scores, axis=-1, keepdims=True))
    expo = jnp.exp(scores - top)
    probs = expo / lax.optimization_barrier(jnp.sum(expo, axis=-1, keepdims=True))
    return jnp.einsum('sqk,skd->sqd', low(probs), values, precision=highest)

def project(inputs, weight):
    return jnp.einsum('sgd,dk->sgk', inputs, weight, precision=highest)

def reference(tokens, cond_embed, caption, clip_len, rope_off, text_len, query_proj, key_proj, value_proj, out_proj, gate_proj, up_proj, down_proj, key_text, value_text, ada_weight, ada_bias, query_gain, key_gain, text_gain, text_gate, cotangent):
    f_type = jnp.float32
    row_index = jnp.arange(GROUP, dtype=jnp.int32)
    starts = jnp.cumsum(clip_len, axis=1) - clip_len
    member = (row_index[None, :, None] >= starts[:, None, :]) & (row_index[None, :, None] < (starts + clip_len)[:, None, :])
    member_int = member.astype(jnp.int32)
    clip_of = lax.optimization_barrier(jnp.sum(member_int * jnp.arange(CLIPS, dtype=jnp.int32)[None, None, :], axis=2))
    position = lax.optimization_barrier(jnp.sum(member_int * (row_index[None, :, None] - starts[:, None, :] + rope_off[:, None, :]), axis=2)).astype(f_type)
    half = HEAD // 2
    inverse = 10000.0 ** (-jnp.arange(half, dtype=f_type) / half)
    angle = position[..., None] * inverse
    cosine = jnp.cos(angle)[:, :, None, :]
    sine = jnp.sin(angle)[:, :, None, :]
    text_index = jnp.arange(CLIPS * TXT, dtype=jnp.int32)
    text_clip = text_index // TXT
    text_pos = text_index - text_clip * TXT
    limit = jnp.take(text_len, text_clip, axis=1)
    text_valid = text_pos[None, :] < limit
    self_mask = clip_of[:, :, None] == clip_of[:, None, :]
    cross_mask = (clip_of[:, :, None] == text_clip[None, None, :]) & text_valid[:, None, :]
    scale = HEAD ** (-0.5)
    cond_f = cond_embed.astype(f_type)
    caption_f = caption.astype(f_type).reshape(N_SEQ, CLIPS * TXT, TXT_D)

    def forward(tokens_f, w_query, w_key, w_value, w_out, w_gate, w_up, w_down, w_ktext, w_vtext, w_ada, b_ada, q_gain, k_gain, t_gain, t_gate):
        silu_cond = low(jax.nn.silu(cond_f))
        modulation = (jnp.einsum('ck,kjd->cjd', silu_cond, w_ada, precision=highest) + b_ada[None]).reshape(N_SEQ, CLIPS, 6, D)

        def token_mod(which):
            return jnp.take_along_axis(modulation[:, :, which, :], clip_of[:, :, None], axis=1)
        inputs = tokens_f.reshape(N_SEQ, GROUP, D)
        modin = low(rms(inputs) * (1.0 + token_mod(1)) + token_mod(0))
        queries = low_back(project(modin, w_query)).reshape(N_SEQ, GROUP, HEADS, HEAD)
        keys = low_back(project(modin, w_key)).reshape(N_SEQ, GROUP, HEADS, HEAD)
        values = low(low_back(project(modin, w_value))).reshape(N_SEQ, GROUP, HEADS, HEAD)
        queries = low(rotate(rms(queries) * q_gain, cosine, sine))
        keys = low(rotate(rms(keys) * k_gain, cosine, sine))
        text_keys = low_back(project(caption_f, w_ktext)).reshape(N_SEQ, CLIPS * TXT, HEADS, HEAD)
        text_keys = low(rms(text_keys) * t_gain)
        text_values = low(low_back(project(caption_f, w_vtext))).reshape(N_SEQ, CLIPS * TXT, HEADS, HEAD)

        def per_head(parts):
            query_one, key_one, value_one, tkey_one, tvalue_one = parts
            return (attend(query_one, key_one, value_one, self_mask, scale), attend(query_one, tkey_one, tvalue_one, cross_mask, scale))
        moved = tuple((jnp.moveaxis(part, 2, 0) for part in (queries, keys, values, text_keys, text_values)))
        self_out, cross_out = lax.map(jax.checkpoint(per_head), moved)
        self_out = jnp.moveaxis(self_out, 0, 2)
        cross_out = jnp.moveaxis(cross_out, 0, 2)
        mixed = low(low_back(self_out) + jnp.tanh(t_gate)[:, None] * low_back(cross_out)).reshape(N_SEQ, GROUP, D)
        attn = low_back(project(mixed, w_out))
        hidden = inputs + token_mod(2) * attn
        ffn_in = low(rms(hidden) * (1.0 + token_mod(4)) + token_mod(3))
        gate_pre = low_back(project(ffn_in, w_gate))
        up_pre = low_back(project(ffn_in, w_up))
        act = low(jax.nn.silu(gate_pre) * up_pre)
        ffn = low_back(project(act, w_down))
        return (hidden + token_mod(5) * ffn).reshape(N_SEQ * GROUP, D)
    primals = tuple((part.astype(f_type) for part in (tokens, query_proj, key_proj, value_proj, out_proj, gate_proj, up_proj, down_proj, key_text, value_text, ada_weight, ada_bias, query_gain, key_gain, text_gain, text_gate)))
    result, pullback = jax.vjp(forward, *primals)
    grads = pullback(cotangent.astype(f_type))
    return (result.astype(jnp.bfloat16), grads[0].astype(jnp.bfloat16), grads[1], grads[2], grads[3], grads[4], grads[5], grads[6], grads[7], grads[8], grads[9], grads[10], grads[11], grads[12], grads[13], grads[14], grads[15])
```

```python
import functools
import math

import jax
import jax.numpy as jnp
from jax import lax
from jax.experimental import pallas as pl
from jax.experimental.pallas import tpu as pltpu
from jax.sharding import PartitionSpec as P

epsilon = 1e-06
f_type = jnp.float32
bf_type = jnp.bfloat16
BLOCK = 256
LANES = 128
HEAD = 64
MASK = -2048.0
EXP_SCALE = HEAD ** -0.5 / math.log(2.0)
VMEM_LIMIT = 56 * 2**20


def dot_nt(a, b):
    return lax.dot_general(a, b, (((1,), (1,)), ((), ())), preferred_element_type=f_type)


def dot_tn(a, b):
    return lax.dot_general(a, b, (((0,), (0,)), ((), ())), preferred_element_type=f_type)


def dot_nn(a, b):
    return jnp.dot(a, b, preferred_element_type=f_type)


def lane_of(shape):
    return lax.broadcasted_iota(jnp.int32, shape, len(shape) - 1)


def head_mean(x):
    r = lax.broadcasted_iota(jnp.int32, (LANES, LANES), 0) // HEAD
    c = lax.broadcasted_iota(jnp.int32, (LANES, LANES), 1) // HEAD
    ones = jnp.where(r == c, 1.0 / HEAD, 0.0).astype(bf_type)
    high = x.astype(bf_type)
    low = (x - high.astype(f_type)).astype(bf_type)
    return dot_nn(high, ones) + dot_nn(low, ones)


def swap_halves(x):
    lanes = lane_of(x.shape)
    up = pltpu.roll(x, LANES - 32, 1)
    down = pltpu.roll(x, 32, 1)
    return jnp.where((lanes % HEAD) < 32, up, down)


def normed(x):
    factor = lax.rsqrt(head_mean(x * x) + epsilon)
    return x * factor, factor


def split_pair(x):
    first = lane_of(x.shape) < HEAD
    zero = jnp.zeros_like(x)
    return jnp.concatenate([jnp.where(first, x, zero), jnp.where(first, zero, x)], axis=0)


def join_pair(x):
    n = x.shape[0] // 2
    first = lane_of((n, LANES)) < HEAD
    return jnp.where(first, x[:n, :LANES], x[n:, :LANES])


def self_kernel(lo, hi, q_ref, k_ref, v_ref, cos_ref, sin_ref, qg_ref, kg_ref, qm_ref, km_ref,
                qrot_ref, krot_ref, o_ref, il_ref, ke, ve, qe, acc):
    n_blocks = q_ref.shape[0] // BLOCK

    def prepare(i, _):
        rows = pl.ds(pl.multiple_of(i * BLOCK, BLOCK), BLOCK)
        cos, sin = cos_ref[rows, :], sin_ref[rows, :]
        for src, gain, dst in ((q_ref, qg_ref, qrot_ref), (k_ref, kg_ref, krot_ref)):
            hat, _f = normed(src[rows, :])
            x = hat * gain[0]
            dst[rows, :] = (x * cos + swap_halves(x) * sin).astype(bf_type)
        ke[rows, :LANES] = krot_ref[rows, :]
        ke[rows, LANES:] = km_ref[rows, :]
        ve[rows, :LANES] = v_ref[rows, :].astype(bf_type)
        ve[rows, LANES:] = jnp.ones((BLOCK, LANES), bf_type)
        return 0

    lax.fori_loop(0, n_blocks, prepare, 0)

    def one(i, _):
        rows = pl.ds(pl.multiple_of(i * BLOCK, BLOCK), BLOCK)
        qe[:, :LANES] = split_pair(qrot_ref[rows, :])
        qm = qm_ref[rows, :]
        qe[:BLOCK, LANES:] = qm
        qe[BLOCK:, LANES:] = qm
        acc[...] = jnp.zeros_like(acc)

        def step(j, _):
            cols = pl.ds(pl.multiple_of(j * BLOCK, BLOCK), BLOCK)
            s = dot_nt(qe[...], ke[cols, :])
            e = jnp.exp2(s * EXP_SCALE).astype(bf_type)
            acc[...] += dot_nn(e, ve[cols, :])
            return 0

        lax.fori_loop(lo[i], hi[i], step, 0)
        inv = join_pair(1.0 / acc[:, LANES:])
        o_ref[rows, :] = join_pair(acc[:, :LANES]) * inv
        il_ref[rows, :] = inv
        return 0

    lax.fori_loop(0, n_blocks, one, 0)


def cross_kernel(clo, chi, qrot_ref, tk_ref, tv_ref, tg_ref, qm_ref, tm_ref, gate_ref, so_ref,
                 mixed_ref, co_ref, cil_ref, tke, tve, qe, acc, *, per_clip):
    n_blocks = qrot_ref.shape[0] // BLOCK
    n_text = tk_ref.shape[0] // BLOCK

    def prepare(i, _):
        rows = pl.ds(pl.multiple_of(i * BLOCK, BLOCK), BLOCK)
        hat, _f = normed(tk_ref[rows, :])
        tke[rows, :LANES] = (hat * tg_ref[0]).astype(bf_type)
        tke[rows, LANES:] = tm_ref[rows, :]
        tve[rows, :LANES] = tv_ref[rows, :].astype(bf_type)
        tve[rows, LANES:] = jnp.ones((BLOCK, LANES), bf_type)
        return 0

    lax.fori_loop(0, n_text, prepare, 0)

    def one(i, _):
        rows = pl.ds(pl.multiple_of(i * BLOCK, BLOCK), BLOCK)
        qe[:, :LANES] = split_pair(qrot_ref[rows, :])
        qm = qm_ref[rows, :]
        qe[:BLOCK, LANES:] = qm
        qe[BLOCK:, LANES:] = qm
        acc[...] = jnp.zeros_like(acc)

        def step(j, _):
            cols = pl.ds(pl.multiple_of(j * per_clip, per_clip), per_clip)
            s = dot_nt(qe[...], tke[cols, :])
            e = jnp.exp2(s * EXP_SCALE).astype(bf_type)
            acc[...] += dot_nn(e, tve[cols, :])
            return 0

        lax.fori_loop(clo[i], chi[i], step, 0)
        inv = join_pair(1.0 / acc[:, LANES:])
        cross = join_pair(acc[:, :LANES]) * inv
        co_ref[rows, :] = cross
        cil_ref[rows, :] = inv
        mixed_ref[rows, :] = (so_ref[rows, :] + gate_ref[0] * cross).astype(bf_type)
        return 0

    lax.fori_loop(0, n_blocks, one, 0)


def back_kernel(lo, hi, clo, chi,
                qrot_ref, krot_ref, q_ref, k_ref, v_ref, tk_ref, tv_ref, o_ref, il_ref, co_ref, cil_ref,
                gm_ref, gate_ref, cos_ref, sin_ref, qg_ref, kg_ref, tg_ref, qm_ref, km_ref, tm_ref,
                gq_ref, gk_ref, gv_ref, gtk_ref, gtv_ref, dqg_ref, dkg_ref, dtg_ref, dgate_ref,
                ke, ve, tke, tve, qe, ge, ce, dq, dk, dv, dtk, dtv, dqa, *, per_clip, scale):
    n_blocks = qrot_ref.shape[0] // BLOCK
    n_text = tk_ref.shape[0] // BLOCK
    marks = jnp.where(lane_of((BLOCK, LANES)) < 2, 1.0, 0.0).astype(bf_type)

    def prepare(i, _):
        rows = pl.ds(pl.multiple_of(i * BLOCK, BLOCK), BLOCK)
        ke[rows, :LANES] = krot_ref[rows, :]
        ke[rows, LANES:] = km_ref[rows, :]
        ve[rows, :LANES] = v_ref[rows, :].astype(bf_type)
        ve[rows, LANES:] = marks
        dk[rows, :] = jnp.zeros((BLOCK, LANES), f_type)
        dv[rows, :] = jnp.zeros((BLOCK, LANES), f_type)
        return 0

    lax.fori_loop(0, n_blocks, prepare, 0)

    def prepare_text(i, _):
        rows = pl.ds(pl.multiple_of(i * BLOCK, BLOCK), BLOCK)
        hat, _f = normed(tk_ref[rows, :])
        tke[rows, :LANES] = (hat * tg_ref[0]).astype(bf_type)
        tke[rows, LANES:] = tm_ref[rows, :]
        tve[rows, :LANES] = tv_ref[rows, :].astype(bf_type)
        tve[rows, LANES:] = marks
        dtk[rows, :] = jnp.zeros((BLOCK, LANES), f_type)
        dtv[rows, :] = jnp.zeros((BLOCK, LANES), f_type)
        return 0

    lax.fori_loop(0, n_text, prepare_text, 0)
    dgate_ref[...] = jnp.zeros_like(dgate_ref)

    def load_grad(dst, grad, out, inv):
        scaled = (grad * inv).astype(bf_type)
        dst[:, :LANES] = split_pair(scaled)
        delta = head_mean(grad * out) * (-HEAD) * inv
        lanes = lane_of((BLOCK, LANES))
        for h in range(2):
            one = jnp.broadcast_to(delta[:, h * HEAD:h * HEAD + 1], (BLOCK, LANES))
            high = one.astype(bf_type)
            low = (one - high.astype(f_type)).astype(bf_type)
            both = jnp.where(lanes == 0, high, jnp.where(lanes == 1, low, jnp.zeros_like(low)))
            dst[h * BLOCK:(h + 1) * BLOCK, LANES:] = both

    def pair_step(cols, keys, values, grads, dkey, dvalue):
        s = dot_nt(keys[cols, :], qe[...])
        e = jnp.exp2(s * EXP_SCALE)
        dd = dot_nt(values[cols, :], grads[...])
        ds = (e * dd).astype(bf_type)
        dkey[cols, :] += dot_nn(ds, qe[:, :LANES])
        dvalue[cols, :] += dot_nn(e.astype(bf_type), grads[:, :LANES])
        dqa[...] += dot_tn(ds, keys[cols, :LANES])

    def one(i, _):
        rows = pl.ds(pl.multiple_of(i * BLOCK, BLOCK), BLOCK)
        qe[:, :LANES] = split_pair(qrot_ref[rows, :])
        qm = qm_ref[rows, :]
        qe[:BLOCK, LANES:] = qm
        qe[BLOCK:, LANES:] = qm
        gm = gm_ref[rows, :].astype(f_type)
        load_grad(ge, gm, o_ref[rows, :], il_ref[rows, :])
        co = co_ref[rows, :]
        load_grad(ce, gm * gate_ref[0], co, cil_ref[rows, :])
        dgate_ref[0] += jnp.sum(gm * co, axis=0, keepdims=True)
        dqa[...] = jnp.zeros_like(dqa)

        def step(j, _):
            pair_step(pl.ds(pl.multiple_of(j * BLOCK, BLOCK), BLOCK), ke, ve, ge, dk, dv)
            return 0

        lax.fori_loop(lo[i], hi[i], step, 0)

        def cross_step(j, _):
            pair_step(pl.ds(pl.multiple_of(j * per_clip, per_clip), per_clip), tke, tve, ce, dtk, dtv)
            return 0

        lax.fori_loop(clo[i], chi[i], cross_step, 0)
        dq[rows, :] = join_pair(dqa[...])
        return 0

    lax.fori_loop(0, n_blocks, one, 0)
    for d in (dqg_ref, dkg_ref, dtg_ref):
        d[...] = jnp.zeros_like(d)

    def finish(i, _):
        rows = pl.ds(pl.multiple_of(i * BLOCK, BLOCK), BLOCK)
        cos, sin = cos_ref[rows, :], sin_ref[rows, :]
        for grad, pre, gain, dgain, dst in ((dq, q_ref, qg_ref, dqg_ref, gq_ref), (dk, k_ref, kg_ref, dkg_ref, gk_ref)):
            g = grad[rows, :] * scale
            g = g * cos - swap_halves(g) * sin
            hat, factor = normed(pre[rows, :])
            dgain[0] += jnp.sum(g * hat, axis=0, keepdims=True)
            g = g * gain[0]
            dst[rows, :] = (factor * (g - hat * head_mean(g * hat))).astype(bf_type)
        gv_ref[rows, :] = dv[rows, :].astype(bf_type)
        return 0

    lax.fori_loop(0, n_blocks, finish, 0)

    def finish_text(i, _):
        rows = pl.ds(pl.multiple_of(i * BLOCK, BLOCK), BLOCK)
        g = dtk[rows, :] * scale
        hat, factor = normed(tk_ref[rows, :])
        dtg_ref[0] += jnp.sum(g * hat, axis=0, keepdims=True)
        g = g * tg_ref[0]
        gtk_ref[rows, :] = (factor * (g - hat * head_mean(g * hat))).astype(bf_type)
        gtv_ref[rows, :] = dtv[rows, :].astype(bf_type)
        return 0

    lax.fori_loop(0, n_text, finish_text, 0)


def pair_rows(n, at=0):
    return pl.BlockSpec((n, LANES), lambda p, *_: (0, at + p))


def shared_rows(n):
    return pl.BlockSpec((n, LANES), lambda p, *_: (0, 0))


ONE_ROW = pl.BlockSpec((1, 1, LANES), lambda p, *_: (p, 0, 0))


def params():
    return pltpu.CompilerParams(vmem_limit_bytes=VMEM_LIMIT, dimension_semantics=("arbitrary",))


def cost(flops, n_bytes, exps):
    return pl.CostEstimate(flops=int(flops), bytes_accessed=int(n_bytes), transcendentals=int(exps))


def self_attention(lo, hi, qkv, cos, sin, qgain, kgain, qmask, kmask):
    group, pairs = qkv.shape[0], qkv.shape[1] // (3 * LANES)
    spec = pltpu.PrefetchScalarGridSpec(
        num_scalar_prefetch=2, grid=(pairs,),
        in_specs=[pair_rows(group), pair_rows(group, pairs), pair_rows(group, 2 * pairs),
                  shared_rows(group), shared_rows(group), ONE_ROW, ONE_ROW, shared_rows(group), shared_rows(group)],
        out_specs=[pair_rows(group)] * 4,
        scratch_shapes=[pltpu.VMEM((group, 2 * LANES), bf_type), pltpu.VMEM((group, 2 * LANES), bf_type),
                        pltpu.VMEM((2 * BLOCK, 2 * LANES), bf_type), pltpu.VMEM((2 * BLOCK, 2 * LANES), f_type)])
    wide = (group, pairs * LANES)
    return pl.pallas_call(
        self_kernel, grid_spec=spec,
        out_shape=[jax.ShapeDtypeStruct(wide, bf_type), jax.ShapeDtypeStruct(wide, bf_type),
                   jax.ShapeDtypeStruct(wide, f_type), jax.ShapeDtypeStruct(wide, f_type)],
        compiler_params=params(), name="self_attention",
        cost_estimate=cost(pairs * group * group * 8 * HEAD, qkv.size * 8, pairs * group * group),
    )(lo, hi, qkv, qkv, qkv, cos, sin, qgain, kgain, qmask, kmask)


def cross_attention(clo, chi, qrot, tkv, tgain, qmask, tmask, gate, self_out, per_clip):
    group, pairs = qrot.shape[0], qrot.shape[1] // LANES
    text = tkv.shape[0]
    spec = pltpu.PrefetchScalarGridSpec(
        num_scalar_prefetch=2, grid=(pairs,),
        in_specs=[pair_rows(group), pair_rows(text), pair_rows(text, pairs), ONE_ROW,
                  shared_rows(group), shared_rows(text), ONE_ROW, pair_rows(group)],
        out_specs=[pair_rows(group)] * 3,
        scratch_shapes=[pltpu.VMEM((text, 2 * LANES), bf_type), pltpu.VMEM((text, 2 * LANES), bf_type),
                        pltpu.VMEM((2 * BLOCK, 2 * LANES), bf_type), pltpu.VMEM((2 * BLOCK, 2 * LANES), f_type)])
    wide = (group, pairs * LANES)
    return pl.pallas_call(
        functools.partial(cross_kernel, per_clip=per_clip), grid_spec=spec,
        out_shape=[jax.ShapeDtypeStruct(wide, bf_type), jax.ShapeDtypeStruct(wide, f_type),
                   jax.ShapeDtypeStruct(wide, f_type)],
        compiler_params=params(), name="cross_attention",
        cost_estimate=cost(pairs * group * per_clip * 16 * HEAD, qrot.size * 14, pairs * group * per_clip),
    )(clo, chi, qrot, tkv, tkv, tgain, qmask, tmask, gate, self_out)


def attention_back(lo, hi, clo, chi, qrot, krot, qkv, tkv, self_out, inv, cross_out, cinv, gmix, gate,
                   cos, sin, qgain, kgain, tgain, qmask, kmask, tmask, per_clip, scale):
    group, pairs = qrot.shape[0], qrot.shape[1] // LANES
    text = tkv.shape[0]
    spec = pltpu.PrefetchScalarGridSpec(
        num_scalar_prefetch=4, grid=(pairs,),
        in_specs=[pair_rows(group), pair_rows(group),
                  pair_rows(group), pair_rows(group, pairs), pair_rows(group, 2 * pairs),
                  pair_rows(text), pair_rows(text, pairs),
                  pair_rows(group), pair_rows(group), pair_rows(group), pair_rows(group),
                  pair_rows(group), ONE_ROW, shared_rows(group), shared_rows(group), ONE_ROW, ONE_ROW, ONE_ROW,
                  shared_rows(group), shared_rows(group), shared_rows(text)],
        out_specs=[pair_rows(group)] * 3 + [pair_rows(text)] * 2 + [ONE_ROW] * 4,
        scratch_shapes=[pltpu.VMEM((group, 2 * LANES), bf_type), pltpu.VMEM((group, 2 * LANES), bf_type),
                        pltpu.VMEM((text, 2 * LANES), bf_type), pltpu.VMEM((text, 2 * LANES), bf_type),
                        pltpu.VMEM((2 * BLOCK, 2 * LANES), bf_type), pltpu.VMEM((2 * BLOCK, 2 * LANES), bf_type),
                        pltpu.VMEM((2 * BLOCK, 2 * LANES), bf_type),
                        pltpu.VMEM((group, LANES), f_type), pltpu.VMEM((group, LANES), f_type),
                        pltpu.VMEM((group, LANES), f_type), pltpu.VMEM((text, LANES), f_type),
                        pltpu.VMEM((text, LANES), f_type), pltpu.VMEM((2 * BLOCK, LANES), f_type)])
    wide, wide_text = (group, pairs * LANES), (text, pairs * LANES)
    row = jax.ShapeDtypeStruct((pairs, 1, LANES), f_type)
    return pl.pallas_call(
        functools.partial(back_kernel, per_clip=per_clip, scale=scale), grid_spec=spec,
        out_shape=[jax.ShapeDtypeStruct(wide, bf_type)] * 3 + [jax.ShapeDtypeStruct(wide_text, bf_type)] * 2 + [row] * 4,
        compiler_params=params(), name="attention_back",
        cost_estimate=cost(pairs * group * group * 20 * HEAD, qkv.size * 12, pairs * group * group),
    )(lo, hi, clo, chi, qrot, krot, qkv, qkv, qkv, tkv, tkv, self_out, inv, cross_out, cinv, gmix, gate,
      cos, sin, qgain, kgain, tgain, qmask, kmask, tmask)


def rms_parts(values):
    factor = lax.rsqrt(jnp.mean(values * values, axis=-1, keepdims=True) + epsilon)
    return (values * factor, factor)


def rms_back(grad, hat, factor):
    return factor * (grad - hat * jnp.mean(grad * hat, axis=-1, keepdims=True))


def pad_lanes(x, width):
    extra = width - x.shape[-1]
    return x if extra == 0 else jnp.pad(x, [(0, 0)] * (x.ndim - 1) + [(0, extra)])


def lane_rows(gain, pairs):
    flat = gain.astype(f_type).reshape(-1)
    return pad_lanes(flat, pairs * LANES).reshape(pairs, 1, LANES)


def body(tokens, cond_embed, caption, clip_len, rope_off, text_len, query_proj, key_proj, value_proj, out_proj,
         gate_proj, up_proj, down_proj, key_text, value_text, ada_weight, ada_bias, query_gain, key_gain,
         text_gain, text_gate, cotangent):
    tp, seq = lax.axis_size("tp"), lax.axis_size("seq")
    me_tp, me_seq = lax.axis_index("tp"), lax.axis_index("seq")
    own = tokens.shape[0]
    group = own * tp
    width = tokens.shape[1]
    clips = cond_embed.shape[0]
    heads = query_gain.shape[0]
    inner = heads * HEAD
    pairs = -(-inner // LANES)
    wide = pairs * LANES
    text = caption.shape[0] * tp
    per_clip = text // clips
    scale = HEAD ** -0.5

    lengths = clip_len[0]
    order = jnp.arange(clips, dtype=jnp.int32)
    ends = jnp.sum(jnp.where(order[None, :] <= order[:, None], lengths[None, :], 0), axis=1)
    starts = ends - lengths
    row = jnp.arange(group, dtype=jnp.int32)
    member = (row[:, None] >= starts[None, :]) & (row[:, None] < ends[None, :])
    member_int = member.astype(jnp.int32)
    position = jnp.sum(member_int * (row[:, None] - starts[None, :] + rope_off[0][None, :]), axis=1).astype(f_type)
    half = HEAD // 2
    inverse = 10000.0 ** (-jnp.arange(half, dtype=f_type) / half)
    angle = position[:, None] * inverse[None, :]
    cos, sin = jnp.cos(angle), jnp.sin(angle)
    cos = jnp.concatenate([cos] * 4, axis=1)
    sin = jnp.concatenate([-sin, sin, -sin, sin], axis=1)
    lanes = jnp.arange(LANES, dtype=jnp.int32)[None, :]
    clip_row = jnp.sum(member_int * jnp.arange(clips, dtype=jnp.int32)[None, :], axis=1)
    same = clip_row[:, None] == lanes
    qmask = jnp.where(same, MASK, 0.0).astype(bf_type)
    kmask = jnp.where(same, 0.0, 1.0).astype(bf_type)
    t_row = jnp.arange(text, dtype=jnp.int32)
    t_clip = t_row // per_clip
    t_limit = jnp.sum((t_clip[:, None] == jnp.arange(clips)[None, :]) * text_len[0][None, :], axis=1)
    t_valid = t_row - t_clip * per_clip < t_limit
    tmask = jnp.where((t_clip[:, None] == lanes) & t_valid[:, None], 0.0, 1.0).astype(bf_type)
    first = jnp.arange(group // BLOCK, dtype=jnp.int32) * BLOCK
    clo = jnp.sum((first[:, None] >= ends[None, :]).astype(jnp.int32), axis=1)
    last = jnp.sum((first[:, None] + (BLOCK - 1) >= ends[None, :]).astype(jnp.int32), axis=1)
    chi = last + 1
    pick = jnp.arange(clips, dtype=jnp.int32)[None, :]
    lo = jnp.sum(jnp.where(pick == clo[:, None], starts[None, :], 0), axis=1) // BLOCK
    hi = (jnp.sum(jnp.where(pick == last[:, None], ends[None, :], 0), axis=1) + BLOCK - 1) // BLOCK
    own_row = me_tp * own + jnp.arange(own, dtype=jnp.int32)
    own_member = ((own_row[:, None] >= starts[None, :]) & (own_row[:, None] < ends[None, :])).astype(f_type)

    silu_cond = jax.nn.silu(cond_embed.astype(f_type)).astype(bf_type)
    mod_local = jnp.einsum("ck,kjd->cjd", silu_cond, ada_weight, preferred_element_type=f_type) + ada_bias.astype(f_type)[None]
    modulation = lax.all_gather(mod_local, "tp", axis=2, tiled=True)

    def token_mod(which):
        return sum(own_member[:, c:c + 1] * modulation[c, which][None, :] for c in range(clips))

    rows_in = tokens.astype(f_type)
    normed_own, factor_own = rms_parts(rows_in)
    modin_own = (normed_own * (1.0 + token_mod(1)) + token_mod(0)).astype(bf_type)
    modin = lax.all_gather(modin_own, "tp", axis=0, tiled=True)
    text_all = lax.all_gather(caption, "tp", axis=0, tiled=True)

    hid = gate_proj.shape[1] // seq
    gate_slice = lax.dynamic_slice_in_dim(gate_proj, me_seq * hid, hid, 1)
    up_slice = lax.dynamic_slice_in_dim(up_proj, me_seq * hid, hid, 1)
    down_slice = lax.dynamic_slice_in_dim(down_proj, me_seq * hid, hid, 0)
    w_gate = lax.all_gather(gate_slice, "tp", axis=1, tiled=True)
    w_up = lax.all_gather(up_slice, "tp", axis=1, tiled=True)
    w_down = lax.all_gather(down_slice, "tp", axis=0, tiled=True)
    cut = width // seq
    out_slice = lax.dynamic_slice_in_dim(out_proj, me_seq * cut, cut, 1)
    w_out = lax.all_gather(lax.all_gather(out_slice, "tp", axis=0, tiled=True), "seq", axis=1, tiled=True)

    grad_y = cotangent.astype(f_type)
    g_ffn = lax.all_gather((token_mod(5) * grad_y).astype(bf_type), "seq", axis=0, tiled=True)

    qkv_weight = jnp.concatenate([pad_lanes(query_proj, wide), pad_lanes(key_proj, wide), pad_lanes(value_proj, wide)], axis=1)
    tkv_weight = jnp.concatenate([pad_lanes(key_text, wide), pad_lanes(value_text, wide)], axis=1)
    qkv = jnp.dot(modin, qkv_weight, preferred_element_type=f_type)
    qg, kg, tg = (lane_rows(g, pairs) for g in (query_gain, key_gain, text_gain))
    tgate = jnp.tanh(text_gate.astype(f_type))
    gate_rows = lane_rows(jnp.broadcast_to(tgate[:, None], (heads, HEAD)), pairs)
    qrot, krot, self_out, inv = self_attention(lo, hi, qkv, cos, sin, qg, kg, qmask, kmask)
    tkv = jnp.dot(text_all, tkv_weight, preferred_element_type=f_type)
    mixed, cross_out, cinv = cross_attention(clo, chi, qrot, tkv, tg, qmask, tmask, gate_rows, self_out, per_clip)

    mixed_own = lax.all_to_all(mixed[:, :inner], "tp", split_axis=0, concat_axis=1, tiled=True)
    attn_own = jnp.dot(mixed_own, w_out, preferred_element_type=f_type)
    hidden_own = rows_in + token_mod(2) * attn_own
    normed_mid, factor_mid = rms_parts(hidden_own)
    ffn_in = lax.all_gather((normed_mid * (1.0 + token_mod(4)) + token_mod(3)).astype(bf_type), "seq", axis=0, tiled=True)
    gate_pre = jnp.dot(ffn_in, w_gate, preferred_element_type=f_type)
    up_pre = jnp.dot(ffn_in, w_up, preferred_element_type=f_type)
    gate_sig = jax.nn.sigmoid(gate_pre)
    gate_silu = gate_pre * gate_sig
    act = (gate_silu * up_pre).astype(bf_type)
    g_act = dot_nt(g_ffn, w_down)
    g_up = (g_act * gate_silu).astype(bf_type)
    g_gate = (g_act * up_pre * gate_sig * (1.0 + gate_pre * (1.0 - gate_sig))).astype(bf_type)
    g_mid = lax.psum_scatter((dot_nt(g_gate, w_gate) + dot_nt(g_up, w_up)).astype(bf_type), "seq", scatter_dimension=0, tiled=True).astype(f_type)
    ffn_own = lax.psum_scatter(jnp.dot(act, w_down, preferred_element_type=f_type).astype(bf_type), "seq", scatter_dimension=0, tiled=True).astype(f_type)
    output = (hidden_own + token_mod(5) * ffn_own).astype(bf_type)

    d_gate = lax.psum_scatter(dot_tn(ffn_in, g_gate).astype(bf_type), "tp", scatter_dimension=1, tiled=True)
    d_up = lax.psum_scatter(dot_tn(ffn_in, g_up).astype(bf_type), "tp", scatter_dimension=1, tiled=True)
    d_down = lax.psum_scatter(dot_tn(act, g_ffn).astype(bf_type), "tp", scatter_dimension=0, tiled=True)
    d_gate = lax.all_to_all(d_gate, "seq", split_axis=0, concat_axis=1, tiled=True).astype(f_type)
    d_up = lax.all_to_all(d_up, "seq", split_axis=0, concat_axis=1, tiled=True).astype(f_type)
    d_down = lax.all_to_all(d_down, "seq", split_axis=1, concat_axis=0, tiled=True).astype(f_type)

    g_hidden = grad_y + rms_back(g_mid * (1.0 + token_mod(4)), normed_mid, factor_mid)
    g_attn = (token_mod(2) * g_hidden).astype(bf_type)
    d_out = lax.psum_scatter(dot_tn(mixed_own, g_attn).astype(bf_type), "seq", scatter_dimension=1, tiled=True)
    d_out = lax.psum_scatter(d_out, "tp", scatter_dimension=0, tiled=True).astype(f_type)
    g_mixed = lax.all_to_all(dot_nt(g_attn, w_out).astype(bf_type), "tp", split_axis=1, concat_axis=0, tiled=True)

    gq, gk, gv, gtk, gtv, dqg, dkg, dtg, dgate = attention_back(
        lo, hi, clo, chi, qrot, krot, qkv, tkv, self_out, inv, cross_out, cinv, pad_lanes(g_mixed, wide), gate_rows,
        cos, sin, qg, kg, tg, qmask, kmask, tmask, per_clip, scale)
    gq, gk, gv, gtk, gtv = (g[:, :inner] for g in (gq, gk, gv, gtk, gtv))
    g_modin = lax.psum_scatter((dot_nt(gq, query_proj) + dot_nt(gk, key_proj) + dot_nt(gv, value_proj)).astype(bf_type),
                               "tp", scatter_dimension=0, tiled=True).astype(f_type)

    def over_seq(grad):
        return lax.psum_scatter(grad.astype(bf_type), "seq", scatter_dimension=0, tiled=True).astype(f_type)

    d_query, d_key, d_value = (over_seq(dot_tn(modin, g)) for g in (gq, gk, gv))
    d_ktext, d_vtext = (over_seq(dot_tn(text_all, g)) for g in (gtk, gtv))
    grad_tokens = (g_hidden + rms_back(g_modin * (1.0 + token_mod(1)), normed_own, factor_own)).astype(bf_type)

    pieces = (g_modin, g_modin * normed_own, g_hidden * attn_own, g_mid, g_mid * normed_mid, grad_y * ffn_own)
    clip_grad = jnp.stack([jnp.stack([jnp.sum(own_member[:, c:c + 1] * p, axis=0) for p in pieces]) for c in range(clips)])
    g_mod = lax.psum_scatter(clip_grad, "tp", scatter_dimension=2, tiled=True)
    every_mod = lax.all_gather(g_mod, "seq", axis=0, tiled=True)
    every_cond = lax.all_gather(silu_cond, "seq", axis=0, tiled=True)
    span = every_cond.shape[1] // seq
    my_cond = lax.dynamic_slice_in_dim(every_cond, me_seq * span, span, 1).astype(f_type)
    d_adaw = jnp.einsum("ck,cjd->kjd", my_cond, every_mod, precision=lax.Precision.HIGHEST)
    d_adab = jnp.sum(every_mod, axis=0)

    def gains(d):
        return d.reshape(-1)[:inner].reshape(heads, HEAD)

    d_tgate = jnp.sum(gains(dgate), axis=1) * (1.0 - tgate * tgate)
    d_qgain, d_kgain, d_tgain, d_tgate = lax.psum((gains(dqg), gains(dkg), gains(dtg), d_tgate), "seq")
    return (output, grad_tokens, d_query, d_key, d_value, d_out, d_gate, d_up, d_down, d_ktext, d_vtext, d_adaw,
            d_adab, d_qgain, d_kgain, d_tgain, d_tgate)


def solution(mesh):
    rows, cols, rep = P(("seq", "tp"), None), P(None, "tp"), P("seq", None)
    flat = P("tp", None)
    in_specs = (rows, rep, rows, rep, rep, rep, cols, cols, cols, flat, cols, cols, flat, cols, cols,
                P(None, None, "tp"), cols, flat, flat, flat, P("tp"), rows)
    grad = P("seq", "tp")
    out_specs = (rows, rows, grad, grad, grad, P("tp", "seq"), grad, grad, P("tp", "seq"), grad, grad,
                 P("seq", None, "tp"), cols, flat, flat, flat, P("tp"))
    return jax.shard_map(body, mesh=mesh, in_specs=in_specs, out_specs=out_specs, check_vma=False)
```

```python
import functools
import math

import jax
import jax.numpy as jnp
from jax import lax
from jax.experimental import pallas as pl
from jax.experimental.pallas import tpu as pltpu
from jax.sharding import PartitionSpec as P

epsilon = 1e-06
f_type = jnp.float32
bf_type = jnp.bfloat16
BLOCK = 256
LANES = 128
HEAD = 64
MASK = -2048.0
EXP_SCALE = HEAD ** -0.5 / math.log(2.0)
VMEM_LIMIT = 56 * 2**20


def dot_nt(a, b):
    return lax.dot_general(a, b, (((1,), (1,)), ((), ())), preferred_element_type=f_type)


def dot_tn(a, b):
    return lax.dot_general(a, b, (((0,), (0,)), ((), ())), preferred_element_type=f_type)


def dot_nn(a, b):
    return jnp.dot(a, b, preferred_element_type=f_type)


def lane_of(shape):
    return lax.broadcasted_iota(jnp.int32, shape, len(shape) - 1)


def head_mean(x):
    r = lax.broadcasted_iota(jnp.int32, (LANES, LANES), 0) // HEAD
    c = lax.broadcasted_iota(jnp.int32, (LANES, LANES), 1) // HEAD
    ones = jnp.where(r == c, 1.0 / HEAD, 0.0).astype(bf_type)
    high = x.astype(bf_type)
    low = (x - high.astype(f_type)).astype(bf_type)
    return dot_nn(high, ones) + dot_nn(low, ones)


def swap_halves(x):
    lanes = lane_of(x.shape)
    up = pltpu.roll(x, LANES - 32, 1)
    down = pltpu.roll(x, 32, 1)
    return jnp.where((lanes % HEAD) < 32, up, down)


def normed(x):
    factor = lax.rsqrt(head_mean(x * x) + epsilon)
    return x * factor, factor


def split_pair(x):
    first = lane_of(x.shape) < HEAD
    zero = jnp.zeros_like(x)
    return jnp.concatenate([jnp.where(first, x, zero), jnp.where(first, zero, x)], axis=0)


def join_pair(x):
    n = x.shape[0] // 2
    first = lane_of((n, LANES)) < HEAD
    return jnp.where(first, x[:n, :LANES], x[n:, :LANES])


def self_kernel(lo, hi, q_ref, k_ref, v_ref, cos_ref, sin_ref, qg_ref, kg_ref, qm_ref, km_ref,
                qrot_ref, krot_ref, o_ref, il_ref, ke, ve, qe, acc):
    n_blocks = q_ref.shape[0] // BLOCK

    def prepare(i, _):
        rows = pl.ds(pl.multiple_of(i * BLOCK, BLOCK), BLOCK)
        cos, sin = cos_ref[rows, :], sin_ref[rows, :]
        for src, gain, dst in ((q_ref, qg_ref, qrot_ref), (k_ref, kg_ref, krot_ref)):
            hat, _f = normed(src[rows, :])
            x = hat * gain[0]
            dst[rows, :] = (x * cos + swap_halves(x) * sin).astype(bf_type)
        ke[rows, :LANES] = krot_ref[rows, :]
        ke[rows, LANES:] = km_ref[rows, :]
        ve[rows, :LANES] = v_ref[rows, :].astype(bf_type)
        ve[rows, LANES:] = jnp.ones((BLOCK, LANES), bf_type)
        return 0

    lax.fori_loop(0, n_blocks, prepare, 0)

    def one(i, _):
        rows = pl.ds(pl.multiple_of(i * BLOCK, BLOCK), BLOCK)
        qe[:, :LANES] = split_pair(qrot_ref[rows, :])
        qm = qm_ref[rows, :]
        qe[:BLOCK, LANES:] = qm
        qe[BLOCK:, LANES:] = qm
        acc[...] = jnp.zeros_like(acc)

        def step(j, _):
            cols = pl.ds(pl.multiple_of(j * BLOCK, BLOCK), BLOCK)
            s = dot_nt(qe[...], ke[cols, :])
            e = jnp.exp2(s * EXP_SCALE).astype(bf_type)
            acc[...] += dot_nn(e, ve[cols, :])
            return 0

        lax.fori_loop(lo[i], hi[i], step, 0)
        inv = join_pair(1.0 / acc[:, LANES:])
        o_ref[rows, :] = join_pair(acc[:, :LANES]) * inv
        il_ref[rows, :] = inv
        return 0

    lax.fori_loop(0, n_blocks, one, 0)


def cross_kernel(clo, chi, qrot_ref, tk_ref, tv_ref, tg_ref, qm_ref, tm_ref, gate_ref, so_ref,
                 mixed_ref, co_ref, cil_ref, tke, tve, qe, acc, *, per_clip):
    n_blocks = qrot_ref.shape[0] // BLOCK
    n_text = tk_ref.shape[0] // BLOCK

    def prepare(i, _):
        rows = pl.ds(pl.multiple_of(i * BLOCK, BLOCK), BLOCK)
        hat, _f = normed(tk_ref[rows, :])
        tke[rows, :LANES] = (hat * tg_ref[0]).astype(bf_type)
        tke[rows, LANES:] = tm_ref[rows, :]
        tve[rows, :LANES] = tv_ref[rows, :].astype(bf_type)
        tve[rows, LANES:] = jnp.ones((BLOCK, LANES), bf_type)
        return 0

    lax.fori_loop(0, n_text, prepare, 0)

    def one(i, _):
        rows = pl.ds(pl.multiple_of(i * BLOCK, BLOCK), BLOCK)
        qe[:, :LANES] = split_pair(qrot_ref[rows, :])
        qm = qm_ref[rows, :]
        qe[:BLOCK, LANES:] = qm
        qe[BLOCK:, LANES:] = qm
        acc[...] = jnp.zeros_like(acc)

        def step(j, _):
            cols = pl.ds(pl.multiple_of(j * per_clip, per_clip), per_clip)
            s = dot_nt(qe[...], tke[cols, :])
            e = jnp.exp2(s * EXP_SCALE).astype(bf_type)
            acc[...] += dot_nn(e, tve[cols, :])
            return 0

        lax.fori_loop(clo[i], chi[i], step, 0)
        inv = join_pair(1.0 / acc[:, LANES:])
        cross = join_pair(acc[:, :LANES]) * inv
        co_ref[rows, :] = cross
        cil_ref[rows, :] = inv
        mixed_ref[rows, :] = (so_ref[rows, :] + gate_ref[0] * cross).astype(bf_type)
        return 0

    lax.fori_loop(0, n_blocks, one, 0)


def back_kernel(lo, hi, clo, chi,
                qrot_ref, krot_ref, q_ref, k_ref, v_ref, tk_ref, tv_ref, o_ref, il_ref, co_ref, cil_ref,
                gm_ref, gate_ref, cos_ref, sin_ref, qg_ref, kg_ref, tg_ref, qm_ref, km_ref, tm_ref,
                gq_ref, gk_ref, gv_ref, gtk_ref, gtv_ref, dqg_ref, dkg_ref, dtg_ref, dgate_ref,
                ke, ve, tke, tve, qe, ge, ce, dq, dk, dv, dtk, dtv, dqa, *, per_clip, scale):
    n_blocks = qrot_ref.shape[0] // BLOCK
    n_text = tk_ref.shape[0] // BLOCK
    marks = jnp.where(lane_of((BLOCK, LANES)) < 2, 1.0, 0.0).astype(bf_type)

    def prepare(i, _):
        rows = pl.ds(pl.multiple_of(i * BLOCK, BLOCK), BLOCK)
        ke[rows, :LANES] = krot_ref[rows, :]
        ke[rows, LANES:] = km_ref[rows, :]
        ve[rows, :LANES] = v_ref[rows, :].astype(bf_type)
        ve[rows, LANES:] = marks
        dk[rows, :] = jnp.zeros((BLOCK, LANES), f_type)
        dv[rows, :] = jnp.zeros((BLOCK, LANES), f_type)
        return 0

    lax.fori_loop(0, n_blocks, prepare, 0)

    def prepare_text(i, _):
        rows = pl.ds(pl.multiple_of(i * BLOCK, BLOCK), BLOCK)
        hat, _f = normed(tk_ref[rows, :])
        tke[rows, :LANES] = (hat * tg_ref[0]).astype(bf_type)
        tke[rows, LANES:] = tm_ref[rows, :]
        tve[rows, :LANES] = tv_ref[rows, :].astype(bf_type)
        tve[rows, LANES:] = marks
        dtk[rows, :] = jnp.zeros((BLOCK, LANES), f_type)
        dtv[rows, :] = jnp.zeros((BLOCK, LANES), f_type)
        return 0

    lax.fori_loop(0, n_text, prepare_text, 0)
    dgate_ref[...] = jnp.zeros_like(dgate_ref)

    def load_grad(dst, grad, out, inv):
        scaled = (grad * inv).astype(bf_type)
        dst[:, :LANES] = split_pair(scaled)
        delta = head_mean(grad * out) * (-HEAD) * inv
        lanes = lane_of((BLOCK, LANES))
        for h in range(2):
            one = jnp.broadcast_to(delta[:, h * HEAD:h * HEAD + 1], (BLOCK, LANES))
            high = one.astype(bf_type)
            low = (one - high.astype(f_type)).astype(bf_type)
            both = jnp.where(lanes == 0, high, jnp.where(lanes == 1, low, jnp.zeros_like(low)))
            dst[h * BLOCK:(h + 1) * BLOCK, LANES:] = both

    def pair_step(cols, keys, values, grads, dkey, dvalue):
        s = dot_nt(keys[cols, :], qe[...])
        e = jnp.exp2(s * EXP_SCALE)
        dd = dot_nt(values[cols, :], grads[...])
        ds = (e * dd).astype(bf_type)
        dkey[cols, :] += dot_nn(ds, qe[:, :LANES])
        dvalue[cols, :] += dot_nn(e.astype(bf_type), grads[:, :LANES])
        dqa[...] += dot_tn(ds, keys[cols, :LANES])

    def one(i, _):
        rows = pl.ds(pl.multiple_of(i * BLOCK, BLOCK), BLOCK)
        qe[:, :LANES] = split_pair(qrot_ref[rows, :])
        qm = qm_ref[rows, :]
        qe[:BLOCK, LANES:] = qm
        qe[BLOCK:, LANES:] = qm
        gm = gm_ref[rows, :].astype(f_type)
        load_grad(ge, gm, o_ref[rows, :], il_ref[rows, :])
        co = co_ref[rows, :]
        load_grad(ce, gm * gate_ref[0], co, cil_ref[rows, :])
        dgate_ref[0] += jnp.sum(gm * co, axis=0, keepdims=True)
        dqa[...] = jnp.zeros_like(dqa)

        def step(j, _):
            pair_step(pl.ds(pl.multiple_of(j * BLOCK, BLOCK), BLOCK), ke, ve, ge, dk, dv)
            return 0

        lax.fori_loop(lo[i], hi[i], step, 0)

        def cross_step(j, _):
            pair_step(pl.ds(pl.multiple_of(j * per_clip, per_clip), per_clip), tke, tve, ce, dtk, dtv)
            return 0

        lax.fori_loop(clo[i], chi[i], cross_step, 0)
        dq[rows, :] = join_pair(dqa[...])
        return 0

    lax.fori_loop(0, n_blocks, one, 0)
    for d in (dqg_ref, dkg_ref, dtg_ref):
        d[...] = jnp.zeros_like(d)

    def finish(i, _):
        rows = pl.ds(pl.multiple_of(i * BLOCK, BLOCK), BLOCK)
        cos, sin = cos_ref[rows, :], sin_ref[rows, :]
        for grad, pre, gain, dgain, dst in ((dq, q_ref, qg_ref, dqg_ref, gq_ref), (dk, k_ref, kg_ref, dkg_ref, gk_ref)):
            g = grad[rows, :] * scale
            g = g * cos - swap_halves(g) * sin
            hat, factor = normed(pre[rows, :])
            dgain[0] += jnp.sum(g * hat, axis=0, keepdims=True)
            g = g * gain[0]
            dst[rows, :] = (factor * (g - hat * head_mean(g * hat))).astype(bf_type)
        gv_ref[rows, :] = dv[rows, :].astype(bf_type)
        return 0

    lax.fori_loop(0, n_blocks, finish, 0)

    def finish_text(i, _):
        rows = pl.ds(pl.multiple_of(i * BLOCK, BLOCK), BLOCK)
        g = dtk[rows, :] * scale
        hat, factor = normed(tk_ref[rows, :])
        dtg_ref[0] += jnp.sum(g * hat, axis=0, keepdims=True)
        g = g * tg_ref[0]
        gtk_ref[rows, :] = (factor * (g - hat * head_mean(g * hat))).astype(bf_type)
        gtv_ref[rows, :] = dtv[rows, :].astype(bf_type)
        return 0

    lax.fori_loop(0, n_text, finish_text, 0)


def pair_rows(n, at=0):
    return pl.BlockSpec((n, LANES), lambda p, *_: (0, at + p))


def shared_rows(n):
    return pl.BlockSpec((n, LANES), lambda p, *_: (0, 0))


ONE_ROW = pl.BlockSpec((1, 1, LANES), lambda p, *_: (p, 0, 0))


def params():
    return pltpu.CompilerParams(vmem_limit_bytes=VMEM_LIMIT, dimension_semantics=("arbitrary",))


def cost(flops, n_bytes, exps):
    return pl.CostEstimate(flops=int(flops), bytes_accessed=int(n_bytes), transcendentals=int(exps))


def self_attention(lo, hi, qkv, cos, sin, qgain, kgain, qmask, kmask):
    group, pairs = qkv.shape[0], qkv.shape[1] // (3 * LANES)
    spec = pltpu.PrefetchScalarGridSpec(
        num_scalar_prefetch=2, grid=(pairs,),
        in_specs=[pair_rows(group), pair_rows(group, pairs), pair_rows(group, 2 * pairs),
                  shared_rows(group), shared_rows(group), ONE_ROW, ONE_ROW, shared_rows(group), shared_rows(group)],
        out_specs=[pair_rows(group)] * 4,
        scratch_shapes=[pltpu.VMEM((group, 2 * LANES), bf_type), pltpu.VMEM((group, 2 * LANES), bf_type),
                        pltpu.VMEM((2 * BLOCK, 2 * LANES), bf_type), pltpu.VMEM((2 * BLOCK, 2 * LANES), f_type)])
    wide = (group, pairs * LANES)
    return pl.pallas_call(
        self_kernel, grid_spec=spec,
        out_shape=[jax.ShapeDtypeStruct(wide, bf_type), jax.ShapeDtypeStruct(wide, bf_type),
                   jax.ShapeDtypeStruct(wide, f_type), jax.ShapeDtypeStruct(wide, f_type)],
        compiler_params=params(), name="self_attention",
        cost_estimate=cost(pairs * group * group * 8 * HEAD, qkv.size * 8, pairs * group * group),
    )(lo, hi, qkv, qkv, qkv, cos, sin, qgain, kgain, qmask, kmask)


def cross_attention(clo, chi, qrot, tkv, tgain, qmask, tmask, gate, self_out, per_clip):
    group, pairs = qrot.shape[0], qrot.shape[1] // LANES
    text = tkv.shape[0]
    spec = pltpu.PrefetchScalarGridSpec(
        num_scalar_prefetch=2, grid=(pairs,),
        in_specs=[pair_rows(group), pair_rows(text), pair_rows(text, pairs), ONE_ROW,
                  shared_rows(group), shared_rows(text), ONE_ROW, pair_rows(group)],
        out_specs=[pair_rows(group)] * 3,
        scratch_shapes=[pltpu.VMEM((text, 2 * LANES), bf_type), pltpu.VMEM((text, 2 * LANES), bf_type),
                        pltpu.VMEM((2 * BLOCK, 2 * LANES), bf_type), pltpu.VMEM((2 * BLOCK, 2 * LANES), f_type)])
    wide = (group, pairs * LANES)
    return pl.pallas_call(
        functools.partial(cross_kernel, per_clip=per_clip), grid_spec=spec,
        out_shape=[jax.ShapeDtypeStruct(wide, bf_type), jax.ShapeDtypeStruct(wide, f_type),
                   jax.ShapeDtypeStruct(wide, f_type)],
        compiler_params=params(), name="cross_attention",
        cost_estimate=cost(pairs * group * per_clip * 16 * HEAD, qrot.size * 14, pairs * group * per_clip),
    )(clo, chi, qrot, tkv, tkv, tgain, qmask, tmask, gate, self_out)


def attention_back(lo, hi, clo, chi, qrot, krot, qkv, tkv, self_out, inv, cross_out, cinv, gmix, gate,
                   cos, sin, qgain, kgain, tgain, qmask, kmask, tmask, per_clip, scale):
    group, pairs = qrot.shape[0], qrot.shape[1] // LANES
    text = tkv.shape[0]
    spec = pltpu.PrefetchScalarGridSpec(
        num_scalar_prefetch=4, grid=(pairs,),
        in_specs=[pair_rows(group), pair_rows(group),
                  pair_rows(group), pair_rows(group, pairs), pair_rows(group, 2 * pairs),
                  pair_rows(text), pair_rows(text, pairs),
                  pair_rows(group), pair_rows(group), pair_rows(group), pair_rows(group),
                  pair_rows(group), ONE_ROW, shared_rows(group), shared_rows(group), ONE_ROW, ONE_ROW, ONE_ROW,
                  shared_rows(group), shared_rows(group), shared_rows(text)],
        out_specs=[pair_rows(group)] * 3 + [pair_rows(text)] * 2 + [ONE_ROW] * 4,
        scratch_shapes=[pltpu.VMEM((group, 2 * LANES), bf_type), pltpu.VMEM((group, 2 * LANES), bf_type),
                        pltpu.VMEM((text, 2 * LANES), bf_type), pltpu.VMEM((text, 2 * LANES), bf_type),
                        pltpu.VMEM((2 * BLOCK, 2 * LANES), bf_type), pltpu.VMEM((2 * BLOCK, 2 * LANES), bf_type),
                        pltpu.VMEM((2 * BLOCK, 2 * LANES), bf_type),
                        pltpu.VMEM((group, LANES), f_type), pltpu.VMEM((group, LANES), f_type),
                        pltpu.VMEM((group, LANES), f_type), pltpu.VMEM((text, LANES), f_type),
                        pltpu.VMEM((text, LANES), f_type), pltpu.VMEM((2 * BLOCK, LANES), f_type)])
    wide, wide_text = (group, pairs * LANES), (text, pairs * LANES)
    row = jax.ShapeDtypeStruct((pairs, 1, LANES), f_type)
    return pl.pallas_call(
        functools.partial(back_kernel, per_clip=per_clip, scale=scale), grid_spec=spec,
        out_shape=[jax.ShapeDtypeStruct(wide, bf_type)] * 3 + [jax.ShapeDtypeStruct(wide_text, bf_type)] * 2 + [row] * 4,
        compiler_params=params(), name="attention_back",
        cost_estimate=cost(pairs * group * group * 20 * HEAD, qkv.size * 12, pairs * group * group),
    )(lo, hi, clo, chi, qrot, krot, qkv, qkv, qkv, tkv, tkv, self_out, inv, cross_out, cinv, gmix, gate,
      cos, sin, qgain, kgain, tgain, qmask, kmask, tmask)


MESH = pl.DeviceIdType.MESH


def meet(peers):
    barrier = pltpu.get_barrier_semaphore()
    count = jnp.int32(0)
    for device, there in peers:
        if there is None:
            pl.semaphore_signal(barrier, inc=1, device_id=device, device_id_type=MESH)
            count += 1
        else:
            @pl.when(there)
            def _(device=device):
                pl.semaphore_signal(barrier, inc=1, device_id=device, device_id_type=MESH)
            count += there.astype(jnp.int32)
    pl.semaphore_wait(barrier, count)


def remote(src, dst, send, recv, device):
    return pltpu.make_async_remote_copy(src_ref=src, dst_ref=dst, send_sem=send, recv_sem=recv,
                                        device_id=device, device_id_type=MESH)


def comm_params(collective_id):
    return pltpu.CompilerParams(vmem_limit_bytes=VMEM_LIMIT, collective_id=collective_id, has_side_effects=True)


def in_vmem(count):
    return [pl.BlockSpec(memory_space=pltpu.VMEM)] * count


def small_gather(arrays, axis, n, collective_id):
    m = len(arrays)

    def kernel(*refs):
        x_refs, o_refs, (send, recv) = refs[:m], refs[m:2 * m], refs[2 * m:]
        me = lax.axis_index(axis)
        others = [lax.rem(me + d, n) for d in range(1, n)]
        meet([({axis: o}, None) for o in others])
        copies = [remote(x_ref, o_ref.at[me], send.at[i, d], recv.at[i, d], {axis: o})
                  for i, (x_ref, o_ref) in enumerate(zip(x_refs, o_refs)) for d, o in enumerate(others)]
        for c in copies:
            c.start()
        for x_ref, o_ref in zip(x_refs, o_refs):
            o_ref[me] = x_ref[...]
        for c in copies:
            c.wait()

    return pl.pallas_call(
        kernel, out_shape=[jax.ShapeDtypeStruct((n, *x.shape), x.dtype) for x in arrays],
        in_specs=in_vmem(m), out_specs=in_vmem(m),
        scratch_shapes=[pltpu.SemaphoreType.DMA((m, n - 1))] * 2,
        compiler_params=comm_params(collective_id), name=f"small_gather_{axis}_{collective_id}")(*arrays)


def gather_project(x, weights, n, collective_id):
    own, width = x.shape
    parts = [w.shape[1] for w in weights]

    def kernel(x_ref, *refs):
        w_refs, (all_ref, y_ref, send, recv) = refs[:len(weights)], refs[len(weights):]
        z = lax.axis_index("tp")
        more, less = z + 1 < n, z > 0
        meet([({"tp": z + 1}, more), ({"tp": z - 1}, less)])

        def rows(shard):
            return pl.ds(pl.multiple_of(shard * own, own), own)

        def copy(way, k, shard):
            ref = all_ref.at[rows(shard)]
            return remote(ref, ref, send.at[way, k], recv.at[way, k], {"tp": z + 1 - 2 * way})

        def multiply(shard):
            block = all_ref[rows(shard), :]
            at = 0
            for w_ref, cols in zip(w_refs, parts):
                y_ref[rows(shard), at:at + cols] = dot_nn(block, w_ref[...])
                at += cols

        all_ref[rows(z), :] = x_ref[...]
        pl.when(more)(lambda: copy(0, 0, z).start())
        pl.when(less)(lambda: copy(1, 0, z).start())
        multiply(z)

        def step(k, _):
            from_left, from_right = z - 1 - k, z + 1 + k
            left, right = from_left >= 0, from_right < n

            @pl.when(left)
            def _():
                copy(0, k, from_left).wait_recv()
                pl.when(more)(lambda: copy(0, k + 1, from_left).start())

            @pl.when(right)
            def _():
                copy(1, k, from_right).wait_recv()
                pl.when(less)(lambda: copy(1, k + 1, from_right).start())

            pl.when(left)(lambda: multiply(from_left))
            pl.when(right)(lambda: multiply(from_right))
            return 0

        lax.fori_loop(0, n - 1, step, 0)

        def sent(k, _):
            pl.when(more & (z - k >= 0))(lambda: copy(0, k, z - k).wait_send())
            pl.when(less & (z + k < n))(lambda: copy(1, k, z + k).wait_send())
            return 0

        lax.fori_loop(0, n - 1, sent, 0)

    total = sum(parts)
    return pl.pallas_call(
        kernel,
        out_shape=[jax.ShapeDtypeStruct((n * own, width), x.dtype), jax.ShapeDtypeStruct((n * own, total), f_type)],
        in_specs=in_vmem(1 + len(weights)), out_specs=in_vmem(2),
        scratch_shapes=[pltpu.SemaphoreType.DMA((2, n))] * 2,
        compiler_params=comm_params(collective_id), name="gather_project",
        cost_estimate=cost(2 * n * own * width * total, 4 * n * own * total, 0))(x, *weights)


def project_scatter(grads, weights, n, collective_id):
    own = grads[0].shape[0] // n
    width = weights[0].shape[0]
    m = len(grads)

    def kernel(*refs):
        g_refs, w_refs = refs[:m], refs[m:2 * m]
        o_ref, out_buf, in_buf, send, recv = refs[2 * m:]
        z = lax.axis_index("tp")
        more, less = z + 1 < n, z > 0
        meet([({"tp": z + 1}, more), ({"tp": z - 1}, less)])

        def rows(shard):
            return pl.ds(pl.multiple_of(shard * own, own), own)

        def partial(shard):
            return sum(dot_nt(g_ref[rows(shard), :], w_ref[...]) for g_ref, w_ref in zip(g_refs, w_refs))

        def copy(way, shard):
            return remote(out_buf.at[shard], in_buf.at[way, shard], send.at[shard], recv.at[way, shard],
                          {"tp": z + 1 - 2 * way})

        def step(t, _):
            right_target, left_target = n - 1 - (t - z), t - (n - 1 - z)

            @pl.when((right_target < n) & (right_target > z))
            def _():
                total = partial(right_target)

                @pl.when(less)
                def _():
                    copy(0, right_target).wait_recv()
                    out_buf[right_target] = (total + in_buf[0, right_target].astype(f_type)).astype(bf_type)

                @pl.when(jnp.logical_not(less))
                def _():
                    out_buf[right_target] = total.astype(bf_type)

                copy(0, right_target).start()

            @pl.when((left_target >= 0) & (left_target < z))
            def _():
                total = partial(left_target)

                @pl.when(more)
                def _():
                    copy(1, left_target).wait_recv()
                    out_buf[left_target] = (total + in_buf[1, left_target].astype(f_type)).astype(bf_type)

                @pl.when(jnp.logical_not(more))
                def _():
                    out_buf[left_target] = total.astype(bf_type)

                copy(1, left_target).start()

            return 0

        lax.fori_loop(0, n - 1, step, 0)
        o_ref[...] = partial(z)

        @pl.when(less)
        def _():
            copy(0, z).wait_recv()
            o_ref[...] += in_buf[0, z].astype(f_type)

        @pl.when(more)
        def _():
            copy(1, z).wait_recv()
            o_ref[...] += in_buf[1, z].astype(f_type)

        def sent(k, _):
            pl.when(k > z)(lambda: copy(0, k).wait_send())
            pl.when(k < z)(lambda: copy(1, k).wait_send())
            return 0

        lax.fori_loop(0, n, sent, 0)

    return pl.pallas_call(
        kernel, out_shape=jax.ShapeDtypeStruct((own, width), f_type),
        in_specs=in_vmem(2 * m), out_specs=in_vmem(1)[0],
        scratch_shapes=[pltpu.VMEM((n, own, width), bf_type), pltpu.VMEM((2, n, own, width), bf_type),
                        pltpu.SemaphoreType.DMA((n,)), pltpu.SemaphoreType.DMA((2, n))],
        compiler_params=comm_params(collective_id), name="project_scatter",
        cost_estimate=cost(2 * n * own * width * sum(w.shape[1] for w in weights), 3 * n * own * width, 0))(*grads, *weights)


def small_exchange(arrays, axis, n, collective_id):
    m = len(arrays)

    def kernel(*refs):
        x_refs, o_refs, (send, recv) = refs[:m], refs[m:2 * m], refs[2 * m:]
        me = lax.axis_index(axis)
        others = [lax.rem(me + d, n) for d in range(1, n)]
        meet([({axis: o}, None) for o in others])
        copies = [remote(x_ref.at[o], o_ref.at[me], send.at[i, d], recv.at[i, d], {axis: o})
                  for i, (x_ref, o_ref) in enumerate(zip(x_refs, o_refs)) for d, o in enumerate(others)]
        for c in copies:
            c.start()
        for x_ref, o_ref in zip(x_refs, o_refs):
            o_ref[me] = x_ref[me]
        for c in copies:
            c.wait()

    return pl.pallas_call(
        kernel, out_shape=[jax.ShapeDtypeStruct(x.shape, x.dtype) for x in arrays],
        in_specs=in_vmem(m), out_specs=in_vmem(m),
        scratch_shapes=[pltpu.SemaphoreType.DMA((m, n - 1))] * 2,
        compiler_params=comm_params(collective_id), name=f"small_exchange_{axis}_{collective_id}")(*arrays)


SIBLING, ALONG_X, ALONG_Y, ACROSS = 1, 2, 4, 6


def flip(s, bit):
    for b in (1, 2, 4):
        if bit & b:
            s = s + b - 2 * b * lax.rem(s // b, 2)
    return s


def plane_ffn(x, slices, g_ffn, collective_id):
    own, width = x.shape
    tp, hid = slices.shape[0], slices.shape[2]
    hidden = tp * hid
    half = own // 2
    n = 8
    tiles = width // hid

    def kernel(x_ref, s_ref, g_ref, all_ref, act_ref, gg_ref, gu_ref, wg_ref, wu_ref, wd_ref, load, send, recv):
        s = lax.axis_index("seq")
        sib, px, py, diag = (flip(s, b) for b in (SIBLING, ALONG_X, ALONG_Y, ACROSS))
        loads = []
        for r in range(tp):
            to = slice(r * hid, (r + 1) * hid)
            loads.append(pltpu.make_async_copy(s_ref.at[r, :width], wg_ref.at[:, to], load.at[len(loads)]))
            loads.append(pltpu.make_async_copy(s_ref.at[r, width:2 * width], wu_ref.at[:, to], load.at[len(loads)]))
            for t in range(tiles):
                loads.append(pltpu.make_async_copy(s_ref.at[r, 2 * width + t * hid:2 * width + (t + 1) * hid],
                                                   wd_ref.at[to, t * hid:(t + 1) * hid], load.at[len(loads)]))
        for c in loads:
            c.start()
        meet([({"seq": d}, None) for d in (sib, px, py)])

        def rows(shard, part=None):
            if part is None:
                return pl.ds(pl.multiple_of(shard * own, own), own)
            return pl.ds(pl.multiple_of(shard * own + part * half, half), half)

        def copy(i, shard, part, to):
            ref = all_ref.at[rows(shard, part)]
            return remote(ref, ref, send.at[i], recv.at[i], {"seq": to})

        all_ref[rows(s), :] = x_ref[...]
        x_a, x_b, y_b, y_a = copy(0, s, 0, px), copy(1, s, 1, px), copy(2, s, 1, py), copy(3, s, 0, py)
        c_own = copy(4, s, None, sib)
        for c in (x_a, y_b, x_b, y_a, c_own):
            c.start()
        for c in loads:
            c.wait()

        def work(shard):
            block = all_ref[rows(shard), :]
            gate = dot_nn(block, wg_ref[...])
            up = dot_nn(block, wu_ref[...])
            g_act = dot_nt(g_ref[rows(shard), :], wd_ref[...])
            sig = jax.nn.sigmoid(gate)
            silu = gate * sig
            act_ref[rows(shard), :] = (silu * up).astype(bf_type)
            gu_ref[rows(shard), :] = (g_act * silu).astype(bf_type)
            gg_ref[rows(shard), :] = (g_act * up * sig * (1.0 + gate * (1.0 - sig))).astype(bf_type)

        work(s)
        c_own.wait_recv()
        x_a.wait_recv()
        y_on = copy(5, px, 0, py)
        y_on.start()
        y_b.wait_recv()
        x_on = copy(6, py, 1, px)
        x_on.start()

        def later(k, _):
            @pl.when(k == 0)
            def _():
                work(sib)
                x_b.wait_recv()
                copy(7, px, None, sib).start()
                y_a.wait_recv()
                copy(8, py, None, sib).start()

            @pl.when(k == 1)
            def _():
                copy(7, px, None, sib).wait_recv()
                copy(8, py, None, sib).wait_recv()

            @pl.when(k == 2)
            def _():
                y_on.wait_recv()
                x_on.wait_recv()
                copy(9, diag, None, sib).start()

            @pl.when(k == 3)
            def _():
                copy(9, diag, None, sib).wait_recv()

            first = jnp.where(k == 0, px, jnp.where(k == 1, flip(px, SIBLING), jnp.where(k == 2, diag, flip(diag, SIBLING))))
            work(first)

            @pl.when(k < 2)
            def _():
                work(jnp.where(k == 0, py, flip(py, SIBLING)))

            return 0

        lax.fori_loop(0, 4, later, 0)
        for c in (x_a, x_b, y_b, y_a, c_own, y_on, x_on, copy(7, px, None, sib), copy(8, py, None, sib), copy(9, diag, None, sib)):
            c.wait_send()

    any_spec = pl.BlockSpec(memory_space=pl.ANY)
    low = jax.ShapeDtypeStruct((n * own, hidden), bf_type)
    return pl.pallas_call(
        kernel, out_shape=[jax.ShapeDtypeStruct((n * own, width), bf_type), low, low, low],
        in_specs=[in_vmem(1)[0], any_spec, in_vmem(1)[0]], out_specs=in_vmem(4),
        scratch_shapes=[pltpu.VMEM((width, hidden), bf_type), pltpu.VMEM((width, hidden), bf_type),
                        pltpu.VMEM((hidden, width), bf_type), pltpu.SemaphoreType.DMA((tp * (2 + tiles),)),
                        pltpu.SemaphoreType.DMA((10,)), pltpu.SemaphoreType.DMA((10,))],
        compiler_params=comm_params(collective_id), name="plane_ffn",
        cost_estimate=cost(6 * n * own * width * hidden, 4 * n * own * width, 0))(x, slices, g_ffn)


def plane_sum(partial_of, own, width, s, refs, store):
    stage, c_in, hop_x, hop_y, in_x, in_y, send, recv = refs
    half = own // 2
    sib, px, py, diag = (flip(s, b) for b in (SIBLING, ALONG_X, ALONG_Y, ACROSS))
    top, bottom = pl.ds(0, half), pl.ds(half, half)

    def to_sibling(i, target):
        stage[i] = partial_of(flip(target, SIBLING)).astype(bf_type)
        c = remote(stage.at[i], c_in.at[i], send.at[i], recv.at[i], {"seq": sib})
        c.start()
        return c

    def hop(i, src, dst, to):
        return remote(src, dst, send.at[i], recv.at[i], {"seq": to})

    c_diag = to_sibling(0, diag)
    mine = partial_of(diag)
    c_x = to_sibling(1, px)
    c_diag.wait_recv()
    stage[4] = (mine + c_in[0].astype(f_type)).astype(bf_type)
    d_y = hop(4, stage.at[4, top], hop_y, py)
    d_x = hop(5, stage.at[4, bottom], hop_x, px)
    d_y.start()
    d_x.start()
    mine = partial_of(px)
    c_y = to_sibling(2, py)
    c_x.wait_recv()
    stage[5, half:, :] = (mine[half:] + c_in[1, half:, :].astype(f_type)).astype(bf_type)
    x_b = hop(6, stage.at[5, bottom], in_x.at[bottom], px)
    x_b.start()
    mine_y = partial_of(py)
    c_own = to_sibling(3, s)
    c_y.wait_recv()
    stage[6, :half, :] = (mine_y[:half] + c_in[2, :half, :].astype(f_type)).astype(bf_type)
    y_a = hop(7, stage.at[6, top], in_y.at[top], py)
    y_a.start()
    d_y.wait_recv()
    stage[5, :half, :] = (mine[:half] + c_in[1, :half, :].astype(f_type) + hop_y[...].astype(f_type)).astype(bf_type)
    x_a = hop(8, stage.at[5, top], in_x.at[top], px)
    x_a.start()
    d_x.wait_recv()
    stage[6, half:, :] = (mine_y[half:] + c_in[2, half:, :].astype(f_type) + hop_x[...].astype(f_type)).astype(bf_type)
    y_b = hop(9, stage.at[6, bottom], in_y.at[bottom], py)
    y_b.start()
    total = partial_of(s)
    c_own.wait_recv()
    total = total + c_in[3].astype(f_type)
    x_b.wait_recv()
    y_a.wait_recv()
    x_a.wait_recv()
    y_b.wait_recv()
    store(total + in_x[...].astype(f_type) + in_y[...].astype(f_type))
    for c in (c_diag, c_x, c_y, c_own, d_y, d_x, x_b, y_a, x_a, y_b):
        c.wait_send()


def plane_sum_scratch(own, width):
    half = own // 2
    return [pltpu.VMEM((7, own, width), bf_type), pltpu.VMEM((4, own, width), bf_type),
            pltpu.VMEM((half, width), bf_type), pltpu.VMEM((half, width), bf_type),
            pltpu.VMEM((own, width), bf_type), pltpu.VMEM((own, width), bf_type),
            pltpu.SemaphoreType.DMA((10,)), pltpu.SemaphoreType.DMA((10,))]


def plane_project_scatter(gg, gu, slices, collective_id):
    n = 8
    own = gg.shape[0] // n
    tp, hid = slices.shape[0], slices.shape[2]
    hidden, width = tp * hid, slices.shape[1] // 3

    def kernel(gg_ref, gu_ref, s_ref, o_ref, wg_ref, wu_ref, load, *refs):
        s = lax.axis_index("seq")
        loads = []
        for r in range(tp):
            to = slice(r * hid, (r + 1) * hid)
            loads.append(pltpu.make_async_copy(s_ref.at[r, :width], wg_ref.at[:, to], load.at[2 * r]))
            loads.append(pltpu.make_async_copy(s_ref.at[r, width:2 * width], wu_ref.at[:, to], load.at[2 * r + 1]))
        for c in loads:
            c.start()
        meet([({"seq": flip(s, b)}, None) for b in (SIBLING, ALONG_X, ALONG_Y)])
        for c in loads:
            c.wait()

        def partial_of(shard):
            rows = pl.ds(pl.multiple_of(shard * own, own), own)
            return dot_nt(gg_ref[rows, :], wg_ref[...]) + dot_nt(gu_ref[rows, :], wu_ref[...])

        def store(total):
            o_ref[...] = total

        plane_sum(partial_of, own, width, s, refs, store)

    return pl.pallas_call(
        kernel, out_shape=jax.ShapeDtypeStruct((own, width), f_type),
        in_specs=in_vmem(2) + [pl.BlockSpec(memory_space=pl.ANY)], out_specs=in_vmem(1)[0],
        scratch_shapes=[pltpu.VMEM((width, hidden), bf_type), pltpu.VMEM((width, hidden), bf_type),
                        pltpu.SemaphoreType.DMA((2 * tp,)), *plane_sum_scratch(own, width)],
        compiler_params=comm_params(collective_id), name="plane_project_scatter",
        cost_estimate=cost(4 * n * own * width * hidden, 4 * n * own * width, 0))(gg, gu, slices)


def plane_gather(view, s, send, recv):
    sib, px, py, diag = (flip(s, b) for b in (SIBLING, ALONG_X, ALONG_Y, ACROSS))

    def copy(i, shard, part, to):
        return remote(view(shard, part), view(shard, part), send.at[i], recv.at[i], {"seq": to})

    x_a, x_b, y_b, y_a = copy(0, s, 0, px), copy(1, s, 1, px), copy(2, s, 1, py), copy(3, s, 0, py)
    c_own, y_on, x_on = copy(4, s, None, sib), copy(5, px, 0, py), copy(6, py, 1, px)
    c_x, c_y, c_diag = copy(7, px, None, sib), copy(8, py, None, sib), copy(9, diag, None, sib)

    def start():
        for c in (x_a, y_b, x_b, y_a, c_own):
            c.start()

    def turn():
        x_a.wait_recv()
        y_on.start()
        y_b.wait_recv()
        x_on.start()

    def share():
        x_b.wait_recv()
        c_x.start()
        y_a.wait_recv()
        c_y.start()

    def last():
        y_on.wait_recv()
        x_on.wait_recv()
        c_diag.start()

    def finish():
        for c in (c_own, c_x, c_y, c_diag):
            c.wait_recv()
        for c in (x_a, x_b, y_b, y_a, c_own, y_on, x_on, c_x, c_y, c_diag):
            c.wait_send()

    return start, turn, share, last, finish


def gather_project_both(x, weights, extra, small, collective_id):
    n = 4
    own, width = x.shape
    parts = [w.shape[1] for w in weights]

    def kernel(x_ref, e_ref, t_ref, *refs):
        w_refs, (all_ref, y_ref, e_all, t_all, send, recv, p_send, p_recv, t_send, t_recv) = refs[:len(weights)], refs[len(weights):]
        z, s = lax.axis_index("tp"), lax.axis_index("seq")
        more, less = z + 1 < n, z > 0
        others = [lax.rem(z + d, n) for d in range(1, n)]
        meet([({"tp": o}, None) for o in others] + [({"seq": flip(s, b)}, None) for b in (SIBLING, ALONG_X, ALONG_Y)])
        smalls = [remote(t_ref, t_all.at[z], t_send.at[d], t_recv.at[d], {"tp": o}) for d, o in enumerate(others)]

        def rows(shard):
            return pl.ds(pl.multiple_of(shard * own, own), own)

        def copy(way, k, shard):
            ref = all_ref.at[rows(shard)]
            return remote(ref, ref, send.at[way, k], recv.at[way, k], {"tp": z + 1 - 2 * way})

        def multiply(shard):
            block = all_ref[rows(shard), :]
            at = 0
            for w_ref, cols in zip(w_refs, parts):
                y_ref[rows(shard), at:at + cols] = dot_nn(block, w_ref[...])
                at += cols

        all_ref[rows(z), :] = x_ref[...]
        pl.when(more)(lambda: copy(0, 0, z).start())
        pl.when(less)(lambda: copy(1, 0, z).start())
        e_all[rows(s), :] = e_ref[...]

        def view(shard, part):
            if part is None:
                return e_all.at[rows(shard)]
            return e_all.at[pl.ds(pl.multiple_of(shard * own + part * (own // 2), own // 2), own // 2)]

        start, turn, share, last, finish = plane_gather(view, s, p_send, p_recv)
        start()
        t_all[z] = t_ref[...]
        multiply(z)
        turn()

        def step(k, _):
            from_left, from_right = z - 1 - k, z + 1 + k
            left, right = from_left >= 0, from_right < n

            @pl.when(left)
            def _():
                copy(0, k, from_left).wait_recv()
                pl.when(more)(lambda: copy(0, k + 1, from_left).start())

            @pl.when(right)
            def _():
                copy(1, k, from_right).wait_recv()
                pl.when(less)(lambda: copy(1, k + 1, from_right).start())

            pl.when(k == 0)(share)

            @pl.when(k == 1)
            def _():
                last()
                for c in smalls:
                    c.start()

            pl.when(left)(lambda: multiply(from_left))
            pl.when(right)(lambda: multiply(from_right))
            return 0

        lax.fori_loop(0, n - 1, step, 0)

        def sent(k, _):
            pl.when(more & (z - k >= 0))(lambda: copy(0, k, z - k).wait_send())
            pl.when(less & (z + k < n))(lambda: copy(1, k, z + k).wait_send())
            return 0

        lax.fori_loop(0, n - 1, sent, 0)
        finish()
        for c in smalls:
            c.wait()

    total = sum(parts)
    return pl.pallas_call(
        kernel,
        out_shape=[jax.ShapeDtypeStruct((n * own, width), x.dtype), jax.ShapeDtypeStruct((n * own, total), f_type),
                   jax.ShapeDtypeStruct((8 * own, width), extra.dtype),
                   jax.ShapeDtypeStruct((n, *small.shape), small.dtype)],
        in_specs=in_vmem(3 + len(weights)), out_specs=in_vmem(4),
        scratch_shapes=[pltpu.SemaphoreType.DMA((2, n))] * 2 + [pltpu.SemaphoreType.DMA((10,))] * 2
        + [pltpu.SemaphoreType.DMA((n - 1,))] * 2,
        compiler_params=comm_params(collective_id), name="gather_project_both",
        cost_estimate=cost(2 * n * own * width * total, 4 * n * own * total, 0))(x, extra, small, *weights)


def scatter_both(grads, weights, act, slices, collective_id):
    n = 4
    own = grads[0].shape[0] // n
    width = weights[0].shape[0]
    m = len(grads)
    tp, hid = slices.shape[0], slices.shape[2]
    hidden = tp * hid
    tiles = width // hid
    half = own // 2

    def kernel(*refs):
        g_refs, w_refs = refs[:m], refs[m:2 * m]
        (act_ref, s_ref, o_ref, f_ref, out_buf, in_buf, send, recv, wd_ref, load,
         stage, c_in, hop_x, hop_y, in_x, in_y, p_send, p_recv, keep) = refs[2 * m:]
        z, s = lax.axis_index("tp"), lax.axis_index("seq")
        more, less = z + 1 < n, z > 0
        loads = []
        for r in range(tp):
            for t in range(tiles):
                loads.append(pltpu.make_async_copy(s_ref.at[r, 2 * width + t * hid:2 * width + (t + 1) * hid],
                                                   wd_ref.at[r * hid:(r + 1) * hid, t * hid:(t + 1) * hid], load.at[len(loads)]))
        for c in loads:
            c.start()
        meet([({"tp": z + 1}, more), ({"tp": z - 1}, less)]
             + [({"seq": flip(s, b)}, None) for b in (SIBLING, ALONG_X, ALONG_Y)])

        def rows(shard):
            return pl.ds(pl.multiple_of(shard * own, own), own)

        def partial(shard):
            return sum(dot_nt(g_ref[rows(shard), :], w_ref[...]) for g_ref, w_ref in zip(g_refs, w_refs))

        def copy(way, shard):
            return remote(out_buf.at[shard], in_buf.at[way, shard], send.at[shard], recv.at[way, shard],
                          {"tp": z + 1 - 2 * way})

        def pass_on(way, target, behind):
            total = partial(target)

            @pl.when(behind)
            def _():
                copy(way, target).wait_recv()
                out_buf[target] = (total + in_buf[way, target].astype(f_type)).astype(bf_type)

            @pl.when(jnp.logical_not(behind))
            def _():
                out_buf[target] = total.astype(bf_type)

            copy(way, target).start()

        sib, px, py, diag = (flip(s, b) for b in (SIBLING, ALONG_X, ALONG_Y, ACROSS))
        top, bottom = pl.ds(0, half), pl.ds(half, half)

        def share_of(shard):
            return dot_nn(act_ref[rows(shard), :], wd_ref[...])

        def sibling(i):
            return remote(stage.at[i], c_in.at[i], p_send.at[i], p_recv.at[i], {"seq": sib})

        def hop(i, src, dst, to):
            return remote(src, dst, p_send.at[i], p_recv.at[i], {"seq": to})

        d_y, d_x = hop(4, stage.at[4, top], hop_y, py), hop(5, stage.at[4, bottom], hop_x, px)
        x_b, y_a = hop(6, stage.at[5, bottom], in_x.at[bottom], px), hop(7, stage.at[6, top], in_y.at[top], py)
        x_a, y_b = hop(8, stage.at[5, top], in_x.at[top], px), hop(9, stage.at[6, bottom], in_y.at[bottom], py)

        def first():
            for c in loads:
                c.wait()
            stage[0] = share_of(flip(diag, SIBLING)).astype(bf_type)
            sibling(0).start()
            stage[1] = share_of(flip(px, SIBLING)).astype(bf_type)
            sibling(1).start()
            stage[2] = share_of(flip(py, SIBLING)).astype(bf_type)
            sibling(2).start()
            stage[3] = share_of(sib).astype(bf_type)
            sibling(3).start()
            mine = share_of(diag)
            sibling(0).wait_recv()
            stage[4] = (mine + c_in[0].astype(f_type)).astype(bf_type)
            d_y.start()
            d_x.start()
            mine = share_of(px)
            sibling(1).wait_recv()
            mine = mine + c_in[1].astype(f_type)
            stage[5, half:, :] = mine[half:].astype(bf_type)
            x_b.start()
            keep[:half, :] = mine[:half]
            mine = share_of(py)
            sibling(2).wait_recv()
            mine = mine + c_in[2].astype(f_type)
            stage[6, :half, :] = mine[:half].astype(bf_type)
            y_a.start()
            keep[half:, :] = mine[half:]

        def second():
            d_y.wait_recv()
            stage[5, :half, :] = (keep[:half, :] + hop_y[...].astype(f_type)).astype(bf_type)
            x_a.start()
            d_x.wait_recv()
            stage[6, half:, :] = (keep[half:, :] + hop_x[...].astype(f_type)).astype(bf_type)
            y_b.start()

        def third():
            total = share_of(s)
            sibling(3).wait_recv()
            for c in (x_b, y_a, x_a, y_b):
                c.wait_recv()
            f_ref[...] = total + c_in[3].astype(f_type) + in_x[...].astype(f_type) + in_y[...].astype(f_type)

        def step(t, _):
            right_target, left_target = n - 1 - (t - z), t - (n - 1 - z)
            pl.when((right_target < n) & (right_target > z))(lambda: pass_on(0, right_target, less))
            pl.when((left_target >= 0) & (left_target < z))(lambda: pass_on(1, left_target, more))
            pl.when(t == 0)(first)
            pl.when(t == 1)(second)
            return 0

        lax.fori_loop(0, n - 1, step, 0)
        third()
        o_ref[...] = partial(z)

        @pl.when(less)
        def _():
            copy(0, z).wait_recv()
            o_ref[...] += in_buf[0, z].astype(f_type)

        @pl.when(more)
        def _():
            copy(1, z).wait_recv()
            o_ref[...] += in_buf[1, z].astype(f_type)

        def sent(k, _):
            pl.when(k > z)(lambda: copy(0, k).wait_send())
            pl.when(k < z)(lambda: copy(1, k).wait_send())
            return 0

        lax.fori_loop(0, n, sent, 0)
        for i in range(4):
            sibling(i).wait_send()
        for c in (d_y, d_x, x_b, y_a, x_a, y_b):
            c.wait_send()

    one = jax.ShapeDtypeStruct((own, width), f_type)
    return pl.pallas_call(
        kernel, out_shape=[one, one],
        in_specs=in_vmem(2 * m + 1) + [pl.BlockSpec(memory_space=pl.ANY)], out_specs=in_vmem(2),
        scratch_shapes=[pltpu.VMEM((n, own, width), bf_type), pltpu.VMEM((2, n, own, width), bf_type),
                        pltpu.SemaphoreType.DMA((n,)), pltpu.SemaphoreType.DMA((2, n)),
                        pltpu.VMEM((hidden, width), bf_type), pltpu.SemaphoreType.DMA((tp * tiles,)),
                        *plane_sum_scratch(own, width), pltpu.VMEM((own, width), f_type)],
        compiler_params=comm_params(collective_id), name="scatter_both",
        cost_estimate=cost(2 * n * own * width * sum(w.shape[1] for w in weights), 3 * n * own * width, 0))(
            *grads, *weights, act, slices)


def exchange_project(mixed, out_rows, collective_id):
    n = 4
    own, inner = mixed.shape[0] // n, mixed.shape[1]
    cut, width = out_rows.shape[1:]

    def kernel(m_ref, w_ref, y_ref, own_ref, w_all, got, send, recv, p_send, p_recv):
        z, s = lax.axis_index("tp"), lax.axis_index("seq")
        others = [lax.rem(z + d, n) for d in range(1, n)]
        meet([({"tp": o}, None) for o in others] + [({"seq": flip(s, b)}, None) for b in (SIBLING, ALONG_X, ALONG_Y)])

        def rows(shard):
            return pl.ds(pl.multiple_of(shard * own, own), own)

        copies = [remote(m_ref.at[rows(o)], got.at[z], send.at[d], recv.at[d], {"tp": o}) for d, o in enumerate(others)]
        for c in copies:
            c.start()
        for t in range(n):
            w_all[t, s] = w_ref[t]

        def view(shard, part):
            if part is None:
                return w_all.at[:, shard]
            return w_all.at[part * (n // 2):(part + 1) * (n // 2), shard]

        start, turn, share, last, finish = plane_gather(view, s, p_send, p_recv)
        start()
        got[z] = m_ref[rows(z), :]
        turn()
        share()
        last()
        for c in copies:
            c.wait()
        finish()
        for t in range(n):
            own_ref[:, t * inner:(t + 1) * inner] = got[t]
            part = dot_nn(got[t], w_all[t].reshape(8 * cut, width))
            if t == 0:
                y_ref[...] = part
            else:
                y_ref[...] += part

    return pl.pallas_call(
        kernel,
        out_shape=[jax.ShapeDtypeStruct((own, width), f_type), jax.ShapeDtypeStruct((own, n * inner), bf_type),
                   jax.ShapeDtypeStruct((n, 8, cut, width), bf_type)],
        in_specs=in_vmem(2), out_specs=in_vmem(3),
        scratch_shapes=[pltpu.VMEM((n, own, inner), bf_type)] + [pltpu.SemaphoreType.DMA((n - 1,))] * 2
        + [pltpu.SemaphoreType.DMA((10,))] * 2,
        compiler_params=comm_params(collective_id), name="exchange_project",
        cost_estimate=cost(2 * own * width * width, 10 * own * width, 0))(mixed, out_rows)


def rms_parts(values):
    factor = lax.rsqrt(jnp.mean(values * values, axis=-1, keepdims=True) + epsilon)
    return (values * factor, factor)


def rms_back(grad, hat, factor):
    return factor * (grad - hat * jnp.mean(grad * hat, axis=-1, keepdims=True))


def pad_lanes(x, width):
    extra = width - x.shape[-1]
    return x if extra == 0 else jnp.pad(x, [(0, 0)] * (x.ndim - 1) + [(0, extra)])


def lane_rows(gain, pairs):
    flat = gain.astype(f_type).reshape(-1)
    return pad_lanes(flat, pairs * LANES).reshape(pairs, 1, LANES)


def body(tokens, cond_embed, caption, clip_len, rope_off, text_len, query_proj, key_proj, value_proj, out_proj,
         gate_proj, up_proj, down_proj, key_text, value_text, ada_weight, ada_bias, query_gain, key_gain,
         text_gain, text_gate, cotangent):
    tp, seq = lax.axis_size("tp"), lax.axis_size("seq")
    me_tp, me_seq = lax.axis_index("tp"), lax.axis_index("seq")
    own = tokens.shape[0]
    group = own * tp
    width = tokens.shape[1]
    clips = cond_embed.shape[0]
    heads = query_gain.shape[0]
    inner = heads * HEAD
    pairs = -(-inner // LANES)
    wide = pairs * LANES
    text = caption.shape[0] * tp
    per_clip = text // clips
    scale = HEAD ** -0.5

    lengths = clip_len[0]
    order = jnp.arange(clips, dtype=jnp.int32)
    ends = jnp.sum(jnp.where(order[None, :] <= order[:, None], lengths[None, :], 0), axis=1)
    starts = ends - lengths
    row = jnp.arange(group, dtype=jnp.int32)
    member = (row[:, None] >= starts[None, :]) & (row[:, None] < ends[None, :])
    member_int = member.astype(jnp.int32)
    position = jnp.sum(member_int * (row[:, None] - starts[None, :] + rope_off[0][None, :]), axis=1).astype(f_type)
    half = HEAD // 2
    inverse = 10000.0 ** (-jnp.arange(half, dtype=f_type) / half)
    angle = position[:, None] * inverse[None, :]
    cos, sin = jnp.cos(angle), jnp.sin(angle)
    cos = jnp.concatenate([cos] * 4, axis=1)
    sin = jnp.concatenate([-sin, sin, -sin, sin], axis=1)
    lanes = jnp.arange(LANES, dtype=jnp.int32)[None, :]
    clip_row = jnp.sum(member_int * jnp.arange(clips, dtype=jnp.int32)[None, :], axis=1)
    same = clip_row[:, None] == lanes
    qmask = jnp.where(same, MASK, 0.0).astype(bf_type)
    kmask = jnp.where(same, 0.0, 1.0).astype(bf_type)
    t_row = jnp.arange(text, dtype=jnp.int32)
    t_clip = t_row // per_clip
    t_limit = jnp.sum((t_clip[:, None] == jnp.arange(clips)[None, :]) * text_len[0][None, :], axis=1)
    t_valid = t_row - t_clip * per_clip < t_limit
    tmask = jnp.where((t_clip[:, None] == lanes) & t_valid[:, None], 0.0, 1.0).astype(bf_type)
    first = jnp.arange(group // BLOCK, dtype=jnp.int32) * BLOCK
    clo = jnp.sum((first[:, None] >= ends[None, :]).astype(jnp.int32), axis=1)
    last = jnp.sum((first[:, None] + (BLOCK - 1) >= ends[None, :]).astype(jnp.int32), axis=1)
    chi = last + 1
    pick = jnp.arange(clips, dtype=jnp.int32)[None, :]
    lo = jnp.sum(jnp.where(pick == clo[:, None], starts[None, :], 0), axis=1) // BLOCK
    hi = (jnp.sum(jnp.where(pick == last[:, None], ends[None, :], 0), axis=1) + BLOCK - 1) // BLOCK
    own_row = me_tp * own + jnp.arange(own, dtype=jnp.int32)
    own_member = ((own_row[:, None] >= starts[None, :]) & (own_row[:, None] < ends[None, :])).astype(f_type)

    cap_cut = caption.shape[1] // 2
    caption_a, cond_embed = lax.optimization_barrier((caption[:, :cap_cut], cond_embed))
    silu_cond = jax.nn.silu(cond_embed.astype(f_type)).astype(bf_type)
    mod_local = jnp.einsum("ck,kjd->cjd", silu_cond, ada_weight, preferred_element_type=f_type) + ada_bias.astype(f_type)[None]
    mod_rows, = small_gather([jnp.pad(mod_local.reshape(clips * 6, -1), ((0, -(clips * 6) % 8), (0, 0)))], "tp", tp, 1)
    cut = out_proj.shape[0] // seq
    out_slice = lax.dynamic_slice_in_dim(out_proj, me_seq * cut, cut, 0)
    modulation = mod_rows.transpose(1, 0, 2).reshape(-1, width)[:clips * 6].reshape(clips, 6, width)

    def token_mod(which):
        return sum(own_member[:, c:c + 1] * modulation[c, which][None, :] for c in range(clips))

    rows_in = tokens.astype(f_type)
    normed_own, factor_own = rms_parts(rows_in)
    modin_own = (normed_own * (1.0 + token_mod(1)) + token_mod(0)).astype(bf_type)
    grad_y = cotangent.astype(f_type)
    g_ffn_own = (token_mod(5) * grad_y).astype(bf_type)
    hid = gate_proj.shape[1] // seq
    planar = seq == 8 and tp == 4 and hid % LANES == 0 and inner % LANES == 0
    qkv_weights = [pad_lanes(w, wide) for w in (query_proj, key_proj, value_proj)]
    text_a = lax.all_gather(caption_a, "tp", axis=0, tiled=True)
    if planar:
        modin, qkv, g_ffn, out_rows = gather_project_both(modin_own, qkv_weights, g_ffn_own, out_slice, 2)
    else:
        modin, qkv = gather_project(modin_own, qkv_weights, tp, 2)
        g_ffn = lax.all_gather(g_ffn_own, "seq", axis=0, tiled=True)
        w_out = lax.all_gather(lax.all_gather(out_slice, "tp"), "seq", axis=1).reshape(width, width)
    caption_b, qkv = lax.optimization_barrier((caption[:, cap_cut:], qkv))
    text_b = lax.all_gather(caption_b, "tp", axis=0, tiled=True)

    gate_slice = lax.dynamic_slice_in_dim(gate_proj, me_seq * hid, hid, 1)
    up_slice = lax.dynamic_slice_in_dim(up_proj, me_seq * hid, hid, 1)
    down_slice = lax.dynamic_slice_in_dim(down_proj, me_seq * hid, hid, 0)
    down_turned = down_slice.reshape(hid, -1, hid).transpose(1, 0, 2).reshape(width, hid)
    slices, text_b = lax.optimization_barrier((jnp.concatenate([gate_slice, up_slice, down_turned], axis=0), text_b))
    slices = lax.all_gather(slices, "tp", axis=0, tiled=False)
    w_gate = slices[:, :width].transpose(1, 0, 2).reshape(width, tp * hid)
    w_up = slices[:, width:2 * width].transpose(1, 0, 2).reshape(width, tp * hid)
    w_down = slices[:, 2 * width:].reshape(tp, -1, hid, hid).transpose(0, 2, 1, 3).reshape(tp * hid, width)
    qg, kg, tg = (lane_rows(g, pairs) for g in (query_gain, key_gain, text_gain))
    tgate = jnp.tanh(text_gate.astype(f_type))
    gate_rows = lane_rows(jnp.broadcast_to(tgate[:, None], (heads, HEAD)), pairs)
    qrot, krot, self_out, inv = self_attention(lo, hi, qkv, cos, sin, qg, kg, qmask, kmask)
    text_weight = jnp.concatenate([pad_lanes(key_text, wide), pad_lanes(value_text, wide)], axis=1)
    tkv = dot_nn(text_a, text_weight[:cap_cut]) + dot_nn(text_b, text_weight[cap_cut:])
    mixed, cross_out, cinv = cross_attention(clo, chi, qrot, tkv, tg, qmask, tmask, gate_rows, self_out, per_clip)

    if planar:
        attn_own, mixed_own, w_out = exchange_project(mixed, out_rows, 6)
        w_out = w_out.reshape(width, width)
    else:
        mixed_own = lax.all_to_all(mixed[:, :inner], "tp", split_axis=0, concat_axis=1, tiled=True)
        attn_own = jnp.dot(mixed_own, w_out, preferred_element_type=f_type)
    hidden_own = rows_in + token_mod(2) * attn_own
    normed_mid, factor_mid = rms_parts(hidden_own)
    ffn_own_in = (normed_mid * (1.0 + token_mod(4)) + token_mod(3)).astype(bf_type)
    if planar:
        ffn_in, act, g_gate, g_up = plane_ffn(ffn_own_in, slices, g_ffn, 4)
        g_mid = plane_project_scatter(g_gate, g_up, slices, 5)
    else:
        ffn_in = lax.all_gather(ffn_own_in, "seq", axis=0, tiled=True)
        gate_pre = jnp.dot(ffn_in, w_gate, preferred_element_type=f_type)
        up_pre = jnp.dot(ffn_in, w_up, preferred_element_type=f_type)
        gate_sig = jax.nn.sigmoid(gate_pre)
        gate_silu = gate_pre * gate_sig
        act = (gate_silu * up_pre).astype(bf_type)
        g_act = dot_nt(g_ffn, w_down)
        g_up = (g_act * gate_silu).astype(bf_type)
        g_gate = (g_act * up_pre * gate_sig * (1.0 + gate_pre * (1.0 - gate_sig))).astype(bf_type)
        g_mid = lax.psum_scatter((dot_nt(g_gate, w_gate) + dot_nt(g_up, w_up)).astype(bf_type), "seq", scatter_dimension=0, tiled=True).astype(f_type)

    g_hidden = grad_y + rms_back(g_mid * (1.0 + token_mod(4)), normed_mid, factor_mid)
    g_attn = (token_mod(2) * g_hidden).astype(bf_type)
    d_out = lax.psum_scatter(dot_tn(mixed_own, g_attn).astype(bf_type), "seq", scatter_dimension=1, tiled=True)
    g_mixed = lax.all_to_all(dot_nt(g_attn, w_out).astype(bf_type), "tp", split_axis=1, concat_axis=0, tiled=True)

    d_ffn = jnp.concatenate([dot_tn(g, x).astype(bf_type).reshape(tp, hid, width)
                             for g, x in ((g_gate, ffn_in), (g_up, ffn_in), (act, g_ffn))], axis=1)
    d_ffn, g_mixed = lax.optimization_barrier((d_ffn, g_mixed))
    d_ffn = lax.psum_scatter(d_ffn, "tp", scatter_dimension=0, tiled=False)
    d_ffn = lax.all_to_all(d_ffn.reshape(3 * hid, seq, width // seq), "seq", split_axis=1, concat_axis=0, tiled=False)
    d_ffn = d_ffn.reshape(seq, 3, hid, width // seq).astype(f_type)
    d_gate, d_up = (d_ffn[:, i].reshape(seq * hid, width // seq).T for i in range(2))
    d_down = d_ffn[:, 2].reshape(seq * hid, width // seq)

    gq, gk, gv, gtk, gtv, dqg, dkg, dtg, dgate = attention_back(
        lo, hi, clo, chi, qrot, krot, qkv, tkv, self_out, inv, cross_out, cinv, pad_lanes(g_mixed, wide), gate_rows,
        cos, sin, qg, kg, tg, qmask, kmask, tmask, per_clip, scale)
    gq, gk, gv, gtk, gtv = (g[:, :inner] for g in (gq, gk, gv, gtk, gtv))

    grads = [dot_tn(modin, g).astype(bf_type) for g in (gq, gk, gv)] + [
        jnp.concatenate([dot_tn(text_a, g), dot_tn(text_b, g)], axis=0).astype(bf_type) for g in (gtk, gtv)]
    merged, gq = lax.optimization_barrier((jnp.concatenate([g.reshape(seq, -1, inner) for g in grads], axis=1), gq))
    merged = lax.psum_scatter(merged, "seq", scatter_dimension=0, tiled=False)
    proj = [query_proj, key_proj, value_proj]
    if planar:
        g_modin, ffn_own = scatter_both([gq, gk, gv], proj, act, slices, 3)
    else:
        g_modin = project_scatter([gq, gk, gv], proj, tp, 3)
        ffn_own = lax.psum_scatter(dot_nn(act, w_down).astype(bf_type), "seq", scatter_dimension=0, tiled=True).astype(f_type)
    output = (hidden_own + token_mod(5) * ffn_own).astype(bf_type)
    rows_q, rows_t = width // seq, caption.shape[1] // seq
    d_query, d_key, d_value = (merged[i * rows_q:(i + 1) * rows_q].astype(f_type) for i in range(3))
    d_ktext, d_vtext = (merged[3 * rows_q + i * rows_t:3 * rows_q + (i + 1) * rows_t].astype(f_type) for i in range(2))
    grad_tokens = (g_hidden + rms_back(g_modin * (1.0 + token_mod(1)), normed_own, factor_own)).astype(bf_type)

    pieces = (g_modin, g_modin * normed_own, g_hidden * attn_own, g_mid, g_mid * normed_mid, grad_y * ffn_own)
    clip_grad = jnp.stack([jnp.stack([jnp.sum(own_member[:, c:c + 1] * p, axis=0) for p in pieces]) for c in range(clips)])
    mod_parts = clip_grad.reshape(clips * 6, tp, width // tp).transpose(1, 0, 2)
    mod_parts = jnp.pad(mod_parts, ((0, 0), (0, -(clips * 6) % 8), (0, 0)))
    if planar:
        mod_parts, d_out = small_exchange([mod_parts, d_out.reshape(tp, -1, d_out.shape[1])], "tp", tp, 7)
        d_out = jnp.sum(d_out.astype(f_type), axis=0)
    else:
        mod_parts, = small_exchange([mod_parts], "tp", tp, 7)
        d_out = lax.psum_scatter(d_out, "tp", scatter_dimension=0, tiled=True).astype(f_type)
    g_mod = jnp.sum(mod_parts, axis=0)

    def gains(d):
        return d.reshape(-1)[:inner].reshape(heads, HEAD)

    row_gate = jnp.sum(gains(dgate), axis=1) * (1.0 - tgate * tgate)
    small = jnp.concatenate([dqg[:, 0], dkg[:, 0], dtg[:, 0], pad_lanes(row_gate[None], LANES)], axis=0)
    small = jnp.pad(small, ((0, -small.shape[0] % 8), (0, 0)))
    cond_rows = jnp.pad(silu_cond, ((0, 16 - clips), (0, 0)))
    every_mod, every_small, every_cond = small_gather([g_mod, small, cond_rows], "seq", seq, 8)
    every_mod = every_mod[:, :clips * 6].reshape(seq * clips, 6, -1)
    every_cond = every_cond[:, :clips].reshape(seq * clips, -1)
    span = every_cond.shape[1] // seq
    my_cond = lax.dynamic_slice_in_dim(every_cond, me_seq * span, span, 1).astype(f_type)
    d_adaw = jnp.einsum("ck,cjd->kjd", my_cond, every_mod, precision=lax.Precision.HIGHEST)
    d_adab = jnp.sum(every_mod, axis=0)
    small = jnp.sum(every_small, axis=0)
    d_qgain, d_kgain, d_tgain = (gains(small[i * pairs:(i + 1) * pairs]) for i in range(3))
    d_tgate = small[3 * pairs, :heads]
    return (output, grad_tokens, d_query, d_key, d_value, d_out, d_gate, d_up, d_down, d_ktext, d_vtext, d_adaw,
            d_adab, d_qgain, d_kgain, d_tgain, d_tgate)


def solution(mesh):
    rows, cols, rep = P(("seq", "tp"), None), P(None, "tp"), P("seq", None)
    flat = P("tp", None)
    in_specs = (rows, rep, rows, rep, rep, rep, cols, cols, cols, flat, cols, cols, flat, cols, cols,
                P(None, None, "tp"), cols, flat, flat, flat, P("tp"), rows)
    grad = P("seq", "tp")
    out_specs = (rows, rows, grad, grad, grad, P("tp", "seq"), grad, grad, P("tp", "seq"), grad, grad,
                 P("seq", None, "tp"), cols, flat, flat, flat, P("tp"))
    return jax.shard_map(body, mesh=mesh, in_specs=in_specs, out_specs=out_specs, check_vma=False)
```
